32 devices in a mesh: gx: 4 (over y, core), gy: 8 (over z, x).
Axes of the slice: x: 2, y: 2, z: 4, core: 2. Of those that a mesh axis runs over, the one named last changes fastest.
Arguments:
- multipoles: float32 [81, 16384], P(None, ('gx', 'gy')), may hold values from -6 to 6
- parent_locals: float32 [81, 2048], P(None, ('gx', 'gy')), may hold values from -6 to 6
- m2l_ops: float32 [81, 81, 256], replicated, may hold values from -0.0625 to 0.0625
- l2l_ops: float32 [8, 81, 81], replicated, may hold values from -0.625 to 0.625
- export_cells: int32 [32, 26, 128], P(('gx', 'gy')), may hold values from 0 to 511
- pair_first: int32 [32, 256, 64], P(('gx', 'gy')), may hold values from 0 to 511
- pair_second: int32 [32, 256, 64], P(('gx', 'gy')), may hold values from 0 to 3839, as said below
- pair_count: int32 [32, 256], P(('gx', 'gy')), may hold values from 32 to 64, as said below
- parent_of: int32 [16384], P(('gx', 'gy')), may hold values from 0 to 2047, as said below
- octant: int32 [16384], P(('gx', 'gy')), may hold values from 0 to 7
Outputs:
- local_expansions: float32 [81, 16384], P(None, ('gx', 'gy'))
The draws below stay inside these ranges and needn't reach their ends.
Inputs may be any that keep to these rules, and one draw needn't show every extreme that they name: `pair_count`: every segment has a translation vector whose 64 slots are all live. `parent_of`: the parent of a cell of segment d lies among parents d * 64 - 16 to (d + 1) * 64 + 15; every segment's first cell takes the lowest of these that exists and its last cell the highest. `pair_second`: a value of 512 or more always names a peer segment that exists.
All inputs are finite; a program needn't handle non-finite values.
Results may differ from the reference program's by a relative error of at most 0.0003.
Values sent between devices are 32-bit elements; how exact they have to be, the bound alone decides.
No kernel may reach another device: no remote copies, remote signals or barrier semaphores. Data moves between devices by JAX's collectives and lax.ppermute only.
A program may use at most 128 MiB of HBM per device.

```python
import jax
import jax.numpy as jnp
from jax import lax

ORDER = 8
COEF = 81
CLASSES = 256
CELL_DEV = 512
REACH = 13
PEERS = 26
CAP = 128
HALO = 16
SLOTS = 64
SEGMENTS = 32
CELLS = 16384
PARENTS = 2048


def draw_pair_count(key, part):
    key = jax.random.fold_in(key, 11)
    key_counts, key_fullest = jax.random.split(key)
    counts = jax.random.randint(key_counts, (SEGMENTS, CLASSES), SLOTS // 2, SLOTS + 1)
    fullest = jax.random.randint(key_fullest, (SEGMENTS, 1), 0, CLASSES)
    class_line = jnp.arange(CLASSES, dtype=jnp.int32)[None, :]
    return jnp.where(class_line == fullest, SLOTS, counts).astype(jnp.int32)


def draw_parent_of(key, part):
    key = jax.random.fold_in(key, 23)
    cell_line = jnp.arange(CELLS, dtype=jnp.int32)
    jitter = jax.random.randint(key, (CELLS,), -HALO, HALO + 1)
    local_cell = cell_line % CELL_DEV
    jitter = jnp.where(local_cell == 0, -HALO, jnp.where(local_cell == CELL_DEV - 1, HALO, jitter))
    return jnp.clip(cell_line // 8 + jitter, 0, PARENTS - 1).astype(jnp.int32)


def draw_pair_second(key, part):
    key = jax.random.fold_in(key, 31)
    key_local, key_flag, key_peer, key_slot = jax.random.split(key, 4)
    shape = (SEGMENTS, CLASSES, SLOTS)
    local_cell = jax.random.randint(key_local, shape, 0, CELL_DEV)
    remote_flag = jax.random.randint(key_flag, shape, 0, 20) < 9
    peer_slot = jax.random.randint(key_peer, shape, 0, PEERS)
    slot_index = jax.random.randint(key_slot, shape, 0, CAP)
    offset = jnp.where(peer_slot < REACH, peer_slot - REACH, peer_slot - REACH + 1)
    segment_line = jnp.arange(SEGMENTS, dtype=jnp.int32)[:, None, None]
    landing = segment_line + offset
    valid = (landing >= 0) & (landing < SEGMENTS)
    peer_slot = jnp.where(valid, peer_slot, PEERS - 1 - peer_slot)
    remote = CELL_DEV + peer_slot * CAP + slot_index
    return jnp.where(remote_flag, remote, local_cell).astype(jnp.int32)


def set_ends(drawn, own_key, least, high):
    longest = drawn.shape.index(max(drawn.shape))
    spots = []
    for shift in (0, 1):
        where = [jax.random.randint(jax.random.fold_in(own_key, axis), (), 0, length) for axis, length in enumerate(drawn.shape)]
        where[longest] = (where[longest] + shift) % drawn.shape[longest]
        spots.append(tuple(where))
    return drawn.at[spots[0]].set(least).at[spots[1]].set(high)


def steps_of(stream_key, extent, cuts, least, high):
    def one(dim, blocks):
        draws = jax.random.uniform(jax.random.fold_in(jax.random.fold_in(stream_key, 6), dim), (blocks,), jnp.float32, least / len(cuts), high / len(cuts))
        return jnp.repeat(jnp.exp(draws), extent[dim] // blocks).reshape((-1,) + (1,) * (len(extent) - dim - 1))

    loudness = one(*cuts[0])
    for cut in cuts[1:]:
        loudness = loudness * one(*cut)
    return loudness


def gaussian(key, dims, width, reach, pieces=(), kind=jnp.bfloat16):
    array = jax.random.normal(key, dims, jnp.float32) * width
    if len(pieces) > 0:
        array = steps_of(key, dims, pieces, -0.22, 0.18) * array
    return jnp.clip(array, min=-reach, max=reach).astype(kind)


def setup_inputs(seed: int = 0) -> dict:
    seeds = jax.random.split(jax.random.key(seed), 11)
    return {
        "multipoles": gaussian(seeds[0], (COEF, CELLS), 1.0, 6.0, ((1, 32),), jnp.float32),
        "parent_locals": gaussian(seeds[1], (COEF, PARENTS), 1.0, 6.0, ((1, 32),), jnp.float32),
        "m2l_ops": gaussian(seeds[2], (COEF, COEF, CLASSES), (COEF * CLASSES // 2) ** -0.5, 0.0625, (), jnp.float32),
        "l2l_ops": gaussian(seeds[3], (8, COEF, COEF), COEF ** -0.5, 0.625, (), jnp.float32),
        "export_cells": set_ends(jax.random.randint(seeds[4], (SEGMENTS, PEERS, CAP), 0, CELL_DEV), jax.random.fold_in(seeds[4], 1), 0, CELL_DEV - 1).astype(jnp.int32),
        "pair_first": set_ends(jax.random.randint(seeds[5], (SEGMENTS, CLASSES, SLOTS), 0, CELL_DEV), jax.random.fold_in(seeds[5], 1), 0, CELL_DEV - 1).astype(jnp.int32),
        "pair_second": draw_pair_second(jax.random.fold_in(seeds[10], 71), 0),
        "pair_count": draw_pair_count(jax.random.fold_in(seeds[10], 71), 0),
        "parent_of": draw_parent_of(jax.random.fold_in(seeds[10], 71), 0),
        "octant": set_ends(jax.random.randint(seeds[9], (CELLS,), 0, 8), jax.random.fold_in(seeds[9], 1), 0, 7).astype(jnp.int32),
    }


def parity(coeff_count):
    coeff_index = jnp.arange(coeff_count, dtype=jnp.int32)
    degree = jnp.zeros((coeff_count,), jnp.int32)
    for degree_step in range(1, ORDER + 1):
        degree = degree + (coeff_index >= degree_step * degree_step).astype(jnp.int32)
    return (1 - 2 * (degree % 2)).astype(jnp.float32)


def reference(multipoles, parent_locals, m2l_ops, l2l_ops, export_cells, pair_first, pair_second, pair_count, parent_of, octant):
    parity_sign = parity(COEF)
    slot_line = jnp.arange(SLOTS, dtype=jnp.int32)

    def one_owner(totals, owner_index):
        target_cell = (pair_first[owner_index] + owner_index * CELL_DEV).astype(jnp.int32)
        raw_second = pair_second[owner_index]
        peer_slot = jnp.clip((raw_second - CELL_DEV) // CAP, 0, PEERS - 1).astype(jnp.int32)
        slot_index = ((raw_second - CELL_DEV) % CAP).astype(jnp.int32)
        offset = jnp.where(peer_slot < REACH, peer_slot - REACH, peer_slot - REACH + 1).astype(jnp.int32)
        peer_index = jnp.clip(owner_index + offset, 0, SEGMENTS - 1).astype(jnp.int32)
        remote_cell = export_cells[peer_index, PEERS - 1 - peer_slot, slot_index] + peer_index * CELL_DEV
        source_cell = jnp.where(raw_second < CELL_DEV, raw_second + owner_index * CELL_DEV, remote_cell).astype(jnp.int32)
        live_mask = (slot_line[None, :] < pair_count[owner_index][:, None]).astype(jnp.float32)
        columns = jnp.concatenate([multipoles[:, source_cell], multipoles[:, target_cell] * parity_sign[:, None, None]], axis=2)
        product = jnp.einsum("ijk,jkq->ikq", m2l_ops, columns, precision=lax.Precision.HIGHEST)
        to_target = product[:, :, :SLOTS] * live_mask
        to_source = product[:, :, SLOTS:] * (live_mask * parity_sign[:, None, None])
        totals = totals.at[:, target_cell].add(to_target)
        totals = totals.at[:, source_cell].add(to_source)
        return totals, None

    near_field, _ = lax.scan(one_owner, jnp.zeros((COEF, CELLS), jnp.float32), jnp.arange(SEGMENTS, dtype=jnp.int32))
    gathered = parent_locals[:, parent_of]
    from_parent = jnp.zeros((COEF, CELLS), jnp.float32)
    for child_octant in range(8):
        octant_term = jnp.dot(l2l_ops[child_octant], gathered, precision=lax.Precision.HIGHEST, preferred_element_type=jnp.float32)
        from_parent = from_parent + jnp.where((octant == child_octant)[None, :], octant_term, 0.0)
    return from_parent + near_field
```

```python
import jax
import jax.numpy as jnp
from jax import lax
from jax.experimental import pallas as pl
from jax.experimental.pallas import tpu as pltpu
from jax.sharding import PartitionSpec as P

ORDER = 8
HALO = 16
LANES = 128
GROUP = 256
ACCS = 8
F32 = jnp.float32
BF16 = jnp.bfloat16
MAT_NT = (((1,), (1,)), ((), ()))


def split(value):
    high = value.astype(BF16)
    return high, (value - high.astype(F32)).astype(BF16)


def dot(a, b):
    return jnp.dot(a, b, preferred_element_type=F32)


def dot_nt(a, b):
    return lax.dot_general(a, b, MAT_NT, preferred_element_type=F32)


def pad_rows(value, rows):
    return jnp.concatenate(
        [value, jnp.zeros((rows - value.shape[0], value.shape[1]), value.dtype)], axis=0
    )


def parity_at(index):
    degree = jnp.zeros_like(index)
    for step in range(1, ORDER + 1):
        degree = degree + (index >= step * step).astype(jnp.int32)
    return (1 - 2 * (degree & 1)).astype(F32)


def peer_offset(slot, reach):
    return slot - reach if slot < reach else slot - reach + 1


def export_kernel(me, devices, reach, x_ref, idx_ref, out_ref):
    coeffs, cells = x_ref.shape
    rows = out_ref.shape[1]
    high, low = split(pad_rows(x_ref[...], rows))
    both = jnp.concatenate([high, low], axis=0)
    peers = idx_ref.shape[0]
    line = lax.broadcasted_iota(jnp.int32, (cells, LANES), 0)
    for slot in range(peers):
        other = me[0] + peer_offset(slot, reach)

        @pl.when(jnp.logical_and(other >= 0, other < devices))
        def _():
            hot = jnp.where(line == idx_ref[slot : slot + 1, :], 1.0, 0.0).astype(BF16)
            sent = dot(both, hot)
            out_ref[other] = sent[:rows] + sent[rows:]


def ops_kernel(m2l_ref, out_ref):
    coeffs = m2l_ref.shape[0]
    pitch = out_ref.shape[0] // LANES
    for i in range(coeffs):
        out_ref[pl.ds(i, LANES, pitch), :] = pad_rows(m2l_ref[i], LANES).T
    for i in range(coeffs, pitch):
        out_ref[pl.ds(i, LANES, pitch), :] = jnp.zeros((LANES, LANES), F32)


def weights_of(w_ref, start, pitch):
    high, low = split(pad_rows(w_ref[pl.ds(start, pitch), :], LANES))
    return jnp.concatenate(
        [jnp.concatenate([high, high], axis=1), jnp.concatenate([low, low], axis=1)], axis=0
    )


def products(columns, w_ref, first, pitch, slots):
    parts = []
    for k in range(GROUP // slots):
        start = pl.multiple_of((first + k) * pitch, 8)
        y = dot_nt(columns[k * slots : (k + 1) * slots], weights_of(w_ref, start, pitch))
        parts.append(y[:, :LANES] + y[:, LANES:])
    return jnp.concatenate(parts, axis=0)


def source_kernel(devices, reach, slots, me, src, x_ref, tgt_ref, w_ref, ret_ref, own_ref, table, bufs, accs):
    step = pl.program_id(0)
    steps = pl.num_programs(0)
    coeffs, cells = x_ref.shape
    groups = tgt_ref.shape[2]
    classes = GROUP // slots
    pitch = w_ref.shape[0] // (groups * classes)

    @pl.when(step == 0)
    def _():
        sign = parity_at(lax.broadcasted_iota(jnp.int32, (coeffs, cells), 0))
        high, low = split(pad_rows(x_ref[...] * sign, LANES).T)
        table[:, :LANES] = high
        table[:, LANES:] = low
        for acc in accs:
            acc[...] = jnp.zeros_like(acc)

    line = lax.broadcasted_iota(jnp.int32, (GROUP, cells), 1)

    def compute(g):
        hot = jnp.where(tgt_ref[0, :, g : g + 1] == line, 1.0, 0.0).astype(BF16)
        columns = dot(hot, table[...]).astype(BF16)
        bufs[g % 2][...] = products(columns, w_ref, g * classes, pitch, slots)

    def scatter(buf, base):
        for q in range(GROUP):
            acc = accs[q % len(accs)]
            row = src[base + q]
            acc[pl.ds(row, 1), :] += buf[q : q + 1, :]

    base = step * (groups * GROUP)
    compute(0)
    for g in range(1, groups):
        compute(g)
        scatter(bufs[(g - 1) % 2], base + (g - 1) * GROUP)
    scatter(bufs[(groups - 1) % 2], base + (groups - 1) * GROUP)

    @pl.when(step == steps - 1)
    def _():
        sign = parity_at(lax.broadcasted_iota(jnp.int32, (LANES, LANES), 1))

        def total(start):
            value = accs[0][start : start + LANES, :]
            for acc in accs[1:]:
                value = value + acc[start : start + LANES, :]
            return value * sign

        for start in range(0, cells, LANES):
            own_ref[start : start + LANES, :] = total(start)
        rows = ret_ref.shape[1]
        for slot in range((accs[0].shape[0] - cells) // LANES):
            other = me[0] + peer_offset(slot, reach)

            @pl.when(jnp.logical_and(other >= 0, other < devices))
            def _():
                ret_ref[other] = total(cells + slot * LANES).T[:rows]


def target_kernel(
    devices, reach, slots, me, src, x_ref, got_ref, tgt_ref, w_ref, own_ref, par_ref, pos_ref, oct_ref, l2l_ref,
    out_ref, table, near, bufs,
):
    step = pl.program_id(0)
    steps = pl.num_programs(0)
    coeffs, cells = x_ref.shape
    groups = tgt_ref.shape[1]
    classes = GROUP // slots
    pitch = w_ref.shape[0] // (groups * classes)

    @pl.when(step == 0)
    def _():
        table[:cells, :] = pad_rows(x_ref[...], LANES).T
        for slot in range((table.shape[0] - cells) // LANES):
            other = jnp.clip(me[0] + peer_offset(slot, reach), 0, devices - 1)
            start = cells + slot * LANES
            table[start : start + LANES, :] = pad_rows(got_ref[other], LANES).T
        near[...] = jnp.zeros_like(near)

    line = lax.broadcasted_iota(jnp.int32, (cells, GROUP), 0)

    def gather(buf, base):
        for q in range(GROUP):
            buf[q : q + 1, :] = table[pl.ds(src[base + q], 1), :]

    def compute(g):
        high, low = split(bufs[g % 2][...])
        y = products(jnp.concatenate([high, low], axis=1), w_ref, g * classes, pitch, slots)
        hot = jnp.where(tgt_ref[0, g : g + 1, :] == line, 1.0, 0.0).astype(BF16)
        near[...] += dot(hot, jnp.concatenate(split(y), axis=1))

    base = step * (groups * GROUP)
    gather(bufs[0], base)
    for g in range(groups):
        if g + 1 < groups:
            gather(bufs[(g + 1) % 2], base + (g + 1) * GROUP)
        compute(g)

    @pl.when(step == steps - 1)
    def _():
        wide = par_ref.shape[1]
        parents = jnp.concatenate(split(pad_rows(par_ref[...], LANES)), axis=0)
        hot = jnp.where(
            pos_ref[...] == lax.broadcasted_iota(jnp.int32, (wide, cells), 0), 1.0, 0.0
        ).astype(BF16)
        picked = dot(parents, hot).astype(BF16)
        total = (near[:, :LANES] + near[:, LANES:] + own_ref[...]).T[:coeffs]
        for k in range(l2l_ref.shape[0]):
            high, low = split(l2l_ref[k])
            filler = jnp.zeros((coeffs, LANES - coeffs), BF16)
            rows = jnp.concatenate([high, filler, high, filler], axis=1)
            term = dot(rows, picked)
            rows = jnp.concatenate([low, filler], axis=1)
            term = term + dot(rows, picked[:LANES])
            total = total + jnp.where(oct_ref[...] == k, term, 0.0)
        out_ref[...] = total


def back_kernel(devices, reach, me, base_ref, got_ref, idx_ref, out_ref, total):
    coeffs, cells = base_ref.shape
    rows = got_ref.shape[1]
    total[...] = jnp.zeros_like(total)
    line = lax.broadcasted_iota(jnp.int32, (cells, LANES), 0)
    for slot in range(idx_ref.shape[0]):
        other = me[0] + peer_offset(slot, reach)

        @pl.when(jnp.logical_and(other >= 0, other < devices))
        def _():
            hot = jnp.where(line == idx_ref[slot : slot + 1, :], 1.0, 0.0).astype(BF16)
            both = jnp.concatenate(split(got_ref[other]), axis=0)
            total[...] += dot_nt(both, hot)

    out_ref[...] = base_ref[...] + total[:coeffs] + total[rows : rows + coeffs]


def padded_2(shard, axis, width):
    size, length = lax.axis_size(axis), shard.shape[1]
    up = [(i, i + 1) for i in range(size - 1)]
    down = [(j, i) for i, j in up]
    before = lax.ppermute(shard[:, length - width :], axis, up)
    after = lax.ppermute(shard[:, :width], axis, down)
    return jnp.concatenate([before, shard, after], axis=1)


def vmem():
    return pl.BlockSpec(memory_space=pltpu.VMEM)


def smem():
    return pl.BlockSpec(memory_space=pltpu.SMEM)


LIMIT = 56 * 1024 * 1024


def shards(
    multipoles, parent_locals, m2l_ops, l2l_ops, export_cells, pair_first, pair_second, pair_count, parent_of, octant
):
    axes = ("gx", "gy")
    coeffs, cells = multipoles.shape
    exported = export_cells[0]
    peers, send = exported.shape
    reach = peers // 2
    classes = m2l_ops.shape[2]
    slots = pair_first.shape[2]
    devices = lax.axis_size("gx") * lax.axis_size("gy")
    position = lax.axis_index("gx") * lax.axis_size("gy") + lax.axis_index("gy")
    me = position.reshape(1).astype(jnp.int32)
    rows = -(-coeffs // 8) * 8
    steps = 16
    groups = classes * slots // (GROUP * steps)

    outgoing = pl.pallas_call(
        lambda me, *refs: export_kernel(me, devices, reach, *refs),
        out_shape=jax.ShapeDtypeStruct((devices, rows, send), F32),
        in_specs=[smem(), vmem(), vmem()],
        out_specs=vmem(),
        compiler_params=pltpu.CompilerParams(vmem_limit_bytes=LIMIT),
        cost_estimate=pl.CostEstimate(flops=10**9, bytes_accessed=2 * 10**6, transcendentals=0),
        name="exports",
    )(me, multipoles, exported)
    arrived = lax.all_to_all(outgoing, axes, 0, 0, tiled=True)
    padded = padded_2(parent_locals, axes, HALO)

    weights = pl.pallas_call(
        ops_kernel,
        out_shape=jax.ShapeDtypeStruct((classes * rows, LANES), F32),
        grid=(classes // LANES,),
        in_specs=[pl.BlockSpec((coeffs, coeffs, LANES), lambda s: (0, 0, s))],
        out_specs=pl.BlockSpec((LANES * rows, LANES), lambda s: (s, 0)),
        compiler_params=pltpu.CompilerParams(vmem_limit_bytes=LIMIT),
        cost_estimate=pl.CostEstimate(flops=10**9, bytes_accessed=20 * 10**6, transcendentals=0),
        name="operators",
    )(m2l_ops)

    live = lax.broadcasted_iota(jnp.int32, (classes, slots), 1) < pair_count[0][:, None]
    target = jnp.where(live, pair_first[0], -1)
    target_rows = target.reshape(steps, groups, GROUP)
    target_columns = jnp.transpose(target_rows, (0, 2, 1))
    source = pair_second[0].reshape(-1)

    w_spec = pl.BlockSpec((groups * GROUP // slots * rows, LANES), lambda s, *_: (s, 0))
    whole = pl.BlockSpec(memory_space=pltpu.VMEM)
    returned, own = pl.pallas_call(
        lambda me, src, x, t, w, r, o, table, b0, b1, *accs: source_kernel(
            devices, reach, slots, me, src, x, t, w, r, o, table, (b0, b1), accs
        ),
        out_shape=(
            jax.ShapeDtypeStruct((devices, rows, send), F32),
            jax.ShapeDtypeStruct((cells, LANES), F32),
        ),
        grid_spec=pltpu.PrefetchScalarGridSpec(
            num_scalar_prefetch=2,
            grid=(steps,),
            in_specs=[whole, pl.BlockSpec((1, GROUP, groups), lambda s, *_: (s, 0, 0)), w_spec],
            out_specs=(whole, whole),
            scratch_shapes=[
                pltpu.VMEM((cells, 2 * LANES), BF16),
                pltpu.VMEM((GROUP, LANES), F32),
                pltpu.VMEM((GROUP, LANES), F32),
            ]
            + [pltpu.VMEM((cells + peers * send, LANES), F32)] * ACCS,
        ),
        compiler_params=pltpu.CompilerParams(vmem_limit_bytes=LIMIT),
        cost_estimate=pl.CostEstimate(flops=20 * 10**9, bytes_accessed=50 * 10**6, transcendentals=0),
        name="to_source",
    )(me, source, multipoles, target_columns, weights)
    back = lax.all_to_all(returned, axes, 0, 0, tiled=True)

    place = (parent_of - position * parent_locals.shape[1] + HALO).reshape(1, cells)
    base = pl.pallas_call(
        lambda *refs: target_kernel(devices, reach, slots, *refs[:14], refs[14:]),
        out_shape=jax.ShapeDtypeStruct((coeffs, cells), F32),
        grid_spec=pltpu.PrefetchScalarGridSpec(
            num_scalar_prefetch=2,
            grid=(steps,),
            in_specs=[whole, whole, pl.BlockSpec((1, groups, GROUP), lambda s, *_: (s, 0, 0)), w_spec]
            + [whole] * 5,
            out_specs=whole,
            scratch_shapes=[
                pltpu.VMEM((cells + peers * send, LANES), F32),
                pltpu.VMEM((cells, 2 * LANES), F32),
                pltpu.VMEM((GROUP, LANES), F32),
                pltpu.VMEM((GROUP, LANES), F32),
            ],
        ),
        compiler_params=pltpu.CompilerParams(vmem_limit_bytes=LIMIT),
        cost_estimate=pl.CostEstimate(flops=20 * 10**9, bytes_accessed=50 * 10**6, transcendentals=0),
        name="to_target",
    )(me, source, multipoles, arrived, target_rows, weights, own, padded, place, octant.reshape(1, cells), l2l_ops)

    return pl.pallas_call(
        lambda me, *refs: back_kernel(devices, reach, me, *refs),
        out_shape=jax.ShapeDtypeStruct((coeffs, cells), F32),
        in_specs=[smem(), vmem(), vmem(), vmem()],
        out_specs=vmem(),
        scratch_shapes=[pltpu.VMEM((2 * rows, cells), F32)],
        compiler_params=pltpu.CompilerParams(vmem_limit_bytes=LIMIT),
        cost_estimate=pl.CostEstimate(flops=10**9, bytes_accessed=2 * 10**6, transcendentals=0),
        name="returned",
    )(me, base, back, exported)


def solution(mesh):
    placed = (
        P(None, ("gx", "gy")),
        P(None, ("gx", "gy")),
        P(),
        P(),
        P(("gx", "gy"), None, None),
        P(("gx", "gy"), None, None),
        P(("gx", "gy"), None, None),
        P(("gx", "gy"), None),
        P(("gx", "gy")),
        P(("gx", "gy")),
    )
    return jax.shard_map(
        shards, mesh=mesh, in_specs=placed, out_specs=P(None, ("gx", "gy")), check_vma=False
    )
```

```python
import jax
import jax.numpy as jnp
from jax import lax
from jax.experimental import pallas as pl
from jax.experimental.pallas import tpu as pltpu
from jax.sharding import PartitionSpec as P

ORDER = 8
HALO = 16
LANES = 128
GROUP = 256
ACCS = 8
F32 = jnp.float32
BF16 = jnp.bfloat16
MAT_NT = (((1,), (1,)), ((), ()))


def split(value):
    high = value.astype(BF16)
    return high, (value - high.astype(F32)).astype(BF16)


def dot(a, b):
    return jnp.dot(a, b, preferred_element_type=F32)


def dot_nt(a, b):
    return lax.dot_general(a, b, MAT_NT, preferred_element_type=F32)


def pad_rows(value, rows):
    return jnp.concatenate(
        [value, jnp.zeros((rows - value.shape[0], value.shape[1]), value.dtype)], axis=0
    )


def parity_at(index):
    degree = jnp.zeros_like(index)
    for step in range(1, ORDER + 1):
        degree = degree + (index >= step * step).astype(jnp.int32)
    return (1 - 2 * (degree & 1)).astype(F32)


def peer_offset(slot, reach):
    return slot - reach if slot < reach else slot - reach + 1


def stacked(value, coeffs):
    head = coeffs - 1
    high = value.astype(BF16).astype(F32)
    low = value - high
    row = lax.broadcasted_iota(jnp.int32, (2 * LANES - 3 * head, value.shape[1]), 0)
    last = jnp.where(row == 1, low[head:], jnp.where(row < 3, high[head:], 0.0))
    return jnp.concatenate([high[:head], low[:head], high[:head], last], axis=0)


def tagged(value, coeffs):
    head = coeffs - 1
    last = value[head : head + 1]
    row = lax.broadcasted_iota(jnp.int32, (LANES - head, value.shape[1]), 0)
    low = last - last.astype(BF16).astype(F32)
    tail = jnp.where(row == 1, low, jnp.where(row < 3, last, 0.0))
    return jnp.concatenate([value[:head], tail], axis=0)


def paired(rows, coeffs):
    head = coeffs - 1
    high = rows.astype(BF16).astype(F32)
    low = pltpu.roll(rows - high, head, 1)
    again = pltpu.roll(high, 2 * head - LANES, 1)
    lane = lax.broadcasted_iota(jnp.int32, rows.shape, 1)
    left = jnp.where(lane < head, high, low)
    right = jnp.where(lane < 2 * head - LANES, low, again)
    return jnp.concatenate([left, right], axis=1).astype(BF16)


def halo_out(rows, coeffs):
    lane = lax.broadcasted_iota(jnp.int32, (1, LANES), 1)
    room = LANES - coeffs
    last = rows[HALO - 1 :]
    first = jnp.where(lane < coeffs, rows[:1], pltpu.roll(last, coeffs, 1))
    second = jnp.where(lane < coeffs, rows[1:2], pltpu.roll(last, coeffs - room, 1))
    return jnp.concatenate([first, second, rows[2 : HALO - 1]], axis=0)


def halo_in(sent, coeffs):
    lane = lax.broadcasted_iota(jnp.int32, (1, LANES), 1)
    room = LANES - coeffs
    last = jnp.where(
        lane < room, pltpu.roll(sent[:1], room, 1), pltpu.roll(sent[1:2], LANES + room - coeffs, 1)
    )
    rows = jnp.concatenate([sent, last], axis=0)
    return jnp.where(lax.broadcasted_iota(jnp.int32, rows.shape, 1) < coeffs, rows, 0.0)


def export_kernel(me, devices, reach, x_ref, idx_ref, par_ref, out_ref):
    coeffs, cells = x_ref.shape
    rows = -(-coeffs // 8) * 8
    high, low = split(pad_rows(x_ref[...], rows))
    both = jnp.concatenate([high, low], axis=0)
    peers = idx_ref.shape[0]
    parents = pad_rows(par_ref[...], LANES).T
    line = lax.broadcasted_iota(jnp.int32, (cells, LANES), 0)
    for slot in range(peers):
        other = me[0] + peer_offset(slot, reach)

        @pl.when(jnp.logical_and(other >= 0, other < devices))
        def _():
            hot = jnp.where(line == idx_ref[slot : slot + 1, :], 1.0, 0.0).astype(BF16)
            sent = dot(both, hot)
            out_ref[other, :rows] = sent[:rows] + sent[rows:]
            if slot == reach - 1:
                out_ref[other, coeffs : coeffs + HALO - 1] = halo_out(parents[:HALO], coeffs)
            if slot == reach:
                out_ref[other, coeffs : coeffs + HALO - 1] = halo_out(parents[-HALO:], coeffs)


def ops_kernel(m2l_ref, out_ref, turned):
    coeffs = m2l_ref.shape[0]
    pitch = out_ref.shape[0] // LANES
    for i in range(coeffs):
        turned[pl.ds(i, pitch, pitch), :] = pad_rows(m2l_ref[i], pitch)
    for j in range(coeffs):
        block = pad_rows(turned[j * pitch : j * pitch + coeffs, :], LANES).T
        out_ref[pl.ds(j, LANES, pitch), :] = block
    out_ref[pl.ds(coeffs, LANES, pitch), :] = block
    out_ref[pl.ds(coeffs + 1, LANES, pitch), :] = block - block.astype(BF16).astype(F32)
    for j in range(coeffs + 2, pitch):
        out_ref[pl.ds(j, LANES, pitch), :] = jnp.zeros((LANES, LANES), F32)


def weights_of(w_ref, start, pitch, coeffs):
    head = coeffs - 1
    high, low = split(w_ref[pl.ds(start, head), :])
    last = pad_rows(w_ref[pl.ds(start + head, pitch - head), :], 2 * LANES - 3 * head).astype(BF16)
    return jnp.concatenate([high, high, low, last], axis=0)


def products(columns, w_ref, first, pitch, slots, coeffs):
    return jnp.concatenate(
        [
            dot(
                columns[k * slots : (k + 1) * slots],
                weights_of(w_ref, (first + k) * pitch, pitch, coeffs),
            )
            for k in range(GROUP // slots)
        ],
        axis=0,
    )


def source_kernel(devices, reach, slots, me, src, x_ref, tgt_ref, w_ref, ret_ref, own_ref, table, bufs, accs):
    step = pl.program_id(0)
    steps = pl.num_programs(0)
    coeffs, cells = x_ref.shape
    groups = tgt_ref.shape[2]
    classes = GROUP // slots
    pitch = w_ref.shape[0] // (groups * classes)

    @pl.when(step == 0)
    def _():
        sign = parity_at(lax.broadcasted_iota(jnp.int32, (coeffs, cells), 0))
        table[...] = stacked(x_ref[...] * sign, coeffs).T.astype(BF16)
        for acc in accs:
            acc[...] = jnp.zeros_like(acc)

    line = lax.broadcasted_iota(jnp.int32, (GROUP, cells), 1)

    def compute(g):
        hot = jnp.where(tgt_ref[0, :, g : g + 1] == line, 1.0, 0.0).astype(BF16)
        columns = dot(hot, table[...]).astype(BF16)
        bufs[g % 2][...] = products(columns, w_ref, g * classes, pitch, slots, coeffs)

    def scatter(buf, base):
        for q in range(GROUP):
            acc = accs[q % len(accs)]
            row = src[base + q]
            acc[pl.ds(row, 1), :] += buf[q : q + 1, :]

    base = step * (groups * GROUP)
    compute(0)
    for g in range(1, groups):
        compute(g)
        scatter(bufs[(g - 1) % 2], base + (g - 1) * GROUP)
    scatter(bufs[(groups - 1) % 2], base + (groups - 1) * GROUP)

    @pl.when(step == steps - 1)
    def _():
        sign = parity_at(lax.broadcasted_iota(jnp.int32, (LANES, LANES), 1))

        def total(start):
            value = accs[0][start : start + LANES, :]
            for acc in accs[1:]:
                value = value + acc[start : start + LANES, :]
            return value * sign

        for start in range(0, cells, LANES):
            own_ref[start : start + LANES, :] = total(start)
        rows = ret_ref.shape[1]
        for slot in range((accs[0].shape[0] - cells) // LANES):
            other = me[0] + peer_offset(slot, reach)

            @pl.when(jnp.logical_and(other >= 0, other < devices))
            def _():
                ret_ref[other] = total(cells + slot * LANES).T[:rows]


def target_kernel(
    devices, reach, slots, me, src, x_ref, got_ref, tgt_ref, w_ref, own_ref, par_ref, pos_ref, oct_ref, l2l_ref,
    out_ref, table, near, bufs,
):
    step = pl.program_id(0)
    steps = pl.num_programs(0)
    coeffs, cells = x_ref.shape
    groups = tgt_ref.shape[1]
    classes = GROUP // slots
    pitch = w_ref.shape[0] // (groups * classes)

    @pl.when(step == 0)
    def _():
        table[:cells, :] = tagged(x_ref[...], coeffs).T
        for slot in range((table.shape[0] - cells) // LANES):
            other = jnp.clip(me[0] + peer_offset(slot, reach), 0, devices - 1)
            start = cells + slot * LANES
            table[start : start + LANES, :] = tagged(got_ref[other, :coeffs], coeffs).T
        near[...] = jnp.zeros_like(near)

    line = lax.broadcasted_iota(jnp.int32, (cells, GROUP), 0)

    def gather(buf, base):
        for q in range(GROUP):
            buf[q : q + 1, :] = table[pl.ds(src[base + q], 1), :]

    def compute(g):
        y = products(paired(bufs[g % 2][...], coeffs), w_ref, g * classes, pitch, slots, coeffs)
        hot = jnp.where(tgt_ref[0, g : g + 1, :] == line, 1.0, 0.0).astype(BF16)
        near[...] += dot(hot, jnp.concatenate(split(y), axis=1))

    base = step * (groups * GROUP)
    gather(bufs[0], base)
    for g in range(groups):
        if g + 1 < groups:
            gather(bufs[(g + 1) % 2], base + (g + 1) * GROUP)
        compute(g)

    @pl.when(step == steps - 1)
    def _():
        parts = [None, pad_rows(par_ref[...], LANES).T, None]
        for part, shift in ((0, -1), (2, 1)):
            other = jnp.clip(me[0] + shift, 0, devices - 1)
            sent = halo_in(got_ref[other, coeffs : coeffs + HALO - 1], coeffs)
            parts[part] = jnp.where(other == me[0], 0.0, sent)
        parents = jnp.concatenate(parts, axis=0)
        wide = parents.shape[0]
        parents = jnp.concatenate(split(parents.T), axis=0)
        hot = jnp.where(
            pos_ref[...] == lax.broadcasted_iota(jnp.int32, (wide, cells), 0), 1.0, 0.0
        ).astype(BF16)
        picked = dot(parents, hot).astype(BF16)
        total = (near[:, :LANES] + near[:, LANES:] + own_ref[...]).T[:coeffs]
        for k in range(l2l_ref.shape[0]):
            high, low = split(l2l_ref[k])
            filler = jnp.zeros((coeffs, LANES - coeffs), BF16)
            rows = jnp.concatenate([high, filler, high, filler], axis=1)
            term = dot(rows, picked)
            rows = jnp.concatenate([low, filler], axis=1)
            term = term + dot(rows, picked[:LANES])
            total = total + jnp.where(oct_ref[...] == k, term, 0.0)
        out_ref[...] = total


def back_kernel(devices, reach, me, base_ref, got_ref, idx_ref, out_ref, total):
    coeffs, cells = base_ref.shape
    rows = got_ref.shape[1]
    total[...] = jnp.zeros_like(total)
    line = lax.broadcasted_iota(jnp.int32, (cells, LANES), 0)
    for slot in range(idx_ref.shape[0]):
        other = me[0] + peer_offset(slot, reach)

        @pl.when(jnp.logical_and(other >= 0, other < devices))
        def _():
            hot = jnp.where(line == idx_ref[slot : slot + 1, :], 1.0, 0.0).astype(BF16)
            both = jnp.concatenate(split(got_ref[other]), axis=0)
            total[...] += dot_nt(both, hot)

    out_ref[...] = base_ref[...] + total[:coeffs] + total[rows : rows + coeffs]


def vmem():
    return pl.BlockSpec(memory_space=pltpu.VMEM)


def smem():
    return pl.BlockSpec(memory_space=pltpu.SMEM)


LIMIT = 56 * 1024 * 1024


def shards(
    multipoles, parent_locals, m2l_ops, l2l_ops, export_cells, pair_first, pair_second, pair_count, parent_of, octant
):
    axes = ("gx", "gy")
    coeffs, cells = multipoles.shape
    exported = export_cells[0]
    peers, send = exported.shape
    reach = peers // 2
    classes = m2l_ops.shape[2]
    slots = pair_first.shape[2]
    devices = lax.axis_size("gx") * lax.axis_size("gy")
    position = lax.axis_index("gx") * lax.axis_size("gy") + lax.axis_index("gy")
    me = position.reshape(1).astype(jnp.int32)
    rows = -(-coeffs // 8) * 8
    steps = 16
    groups = classes * slots // (GROUP * steps)

    outgoing = pl.pallas_call(
        lambda me, *refs: export_kernel(me, devices, reach, *refs),
        out_shape=jax.ShapeDtypeStruct((devices, coeffs + HALO - 1, send), F32),
        in_specs=[smem(), vmem(), vmem(), vmem()],
        out_specs=vmem(),
        compiler_params=pltpu.CompilerParams(vmem_limit_bytes=LIMIT),
        cost_estimate=pl.CostEstimate(flops=10**9, bytes_accessed=2 * 10**6, transcendentals=0),
        name="exports",
    )(me, multipoles, exported, parent_locals)
    arrived = lax.all_to_all(outgoing, axes, 0, 0, tiled=True)

    weights = pl.pallas_call(
        ops_kernel,
        out_shape=jax.ShapeDtypeStruct((classes * rows, LANES), F32),
        grid=(classes // LANES,),
        in_specs=[pl.BlockSpec((coeffs, coeffs, LANES), lambda s: (0, 0, s))],
        out_specs=pl.BlockSpec((LANES * rows, LANES), lambda s: (s, 0)),
        scratch_shapes=[pltpu.VMEM((rows * rows, LANES), F32)],
        compiler_params=pltpu.CompilerParams(vmem_limit_bytes=LIMIT),
        cost_estimate=pl.CostEstimate(flops=10**9, bytes_accessed=20 * 10**6, transcendentals=0),
        name="operators",
    )(m2l_ops)

    live = lax.broadcasted_iota(jnp.int32, (classes, slots), 1) < pair_count[0][:, None]
    target = jnp.where(live, pair_first[0], -1)
    target_rows = target.reshape(steps, groups, GROUP)
    target_columns = jnp.transpose(target_rows, (0, 2, 1))
    source = pair_second[0].reshape(-1)

    w_spec = pl.BlockSpec((groups * GROUP // slots * rows, LANES), lambda s, *_: (s, 0))
    whole = pl.BlockSpec(memory_space=pltpu.VMEM)
    returned, own = pl.pallas_call(
        lambda me, src, x, t, w, r, o, table, b0, b1, *accs: source_kernel(
            devices, reach, slots, me, src, x, t, w, r, o, table, (b0, b1), accs
        ),
        out_shape=(
            jax.ShapeDtypeStruct((devices, rows, send), F32),
            jax.ShapeDtypeStruct((cells, LANES), F32),
        ),
        grid_spec=pltpu.PrefetchScalarGridSpec(
            num_scalar_prefetch=2,
            grid=(steps,),
            in_specs=[whole, pl.BlockSpec((1, GROUP, groups), lambda s, *_: (s, 0, 0)), w_spec],
            out_specs=(whole, whole),
            scratch_shapes=[
                pltpu.VMEM((cells, 2 * LANES), BF16),
                pltpu.VMEM((GROUP, LANES), F32),
                pltpu.VMEM((GROUP, LANES), F32),
            ]
            + [pltpu.VMEM((cells + peers * send, LANES), F32)] * ACCS,
        ),
        compiler_params=pltpu.CompilerParams(vmem_limit_bytes=LIMIT),
        cost_estimate=pl.CostEstimate(flops=20 * 10**9, bytes_accessed=50 * 10**6, transcendentals=0),
        name="to_source",
    )(me, source, multipoles, target_columns, weights)
    back = lax.all_to_all(returned, axes, 0, 0, tiled=True)

    place = (parent_of - position * parent_locals.shape[1] + HALO).reshape(1, cells)
    base = pl.pallas_call(
        lambda *refs: target_kernel(devices, reach, slots, *refs[:14], refs[14:]),
        out_shape=jax.ShapeDtypeStruct((coeffs, cells), F32),
        grid_spec=pltpu.PrefetchScalarGridSpec(
            num_scalar_prefetch=2,
            grid=(steps,),
            in_specs=[whole, whole, pl.BlockSpec((1, groups, GROUP), lambda s, *_: (s, 0, 0)), w_spec]
            + [whole] * 5,
            out_specs=whole,
            scratch_shapes=[
                pltpu.VMEM((cells + peers * send, LANES), F32),
                pltpu.VMEM((cells, 2 * LANES), F32),
                pltpu.VMEM((GROUP, LANES), F32),
                pltpu.VMEM((GROUP, LANES), F32),
            ],
        ),
        compiler_params=pltpu.CompilerParams(vmem_limit_bytes=LIMIT),
        cost_estimate=pl.CostEstimate(flops=20 * 10**9, bytes_accessed=50 * 10**6, transcendentals=0),
        name="to_target",
    )(me, source, multipoles, arrived, target_rows, weights, own, parent_locals, place, octant.reshape(1, cells), l2l_ops)

    return pl.pallas_call(
        lambda me, *refs: back_kernel(devices, reach, me, *refs),
        out_shape=jax.ShapeDtypeStruct((coeffs, cells), F32),
        in_specs=[smem(), vmem(), vmem(), vmem()],
        out_specs=vmem(),
        scratch_shapes=[pltpu.VMEM((2 * rows, cells), F32)],
        compiler_params=pltpu.CompilerParams(vmem_limit_bytes=LIMIT),
        cost_estimate=pl.CostEstimate(flops=10**9, bytes_accessed=2 * 10**6, transcendentals=0),
        name="returned",
    )(me, base, back, exported)


def solution(mesh):
    placed = (
        P(None, ("gx", "gy")),
        P(None, ("gx", "gy")),
        P(),
        P(),
        P(("gx", "gy"), None, None),
        P(("gx", "gy"), None, None),
        P(("gx", "gy"), None, None),
        P(("gx", "gy"), None),
        P(("gx", "gy")),
        P(("gx", "gy")),
    )
    return jax.shard_map(
        shards, mesh=mesh, in_specs=placed, out_specs=P(None, ("gx", "gy")), check_vma=False
    )
```

```python
import jax
import jax.numpy as jnp
from jax import lax
from jax.experimental import pallas as pl
from jax.experimental.pallas import tpu as pltpu
from jax.sharding import PartitionSpec as P

ORDER = 8
HALO = 16
LANES = 128
GROUP = 256
ACCS = 8
F32 = jnp.float32
BF16 = jnp.bfloat16
MAT_NT = (((1,), (1,)), ((), ()))


def split(value):
    high = value.astype(BF16)
    return high, (value - high.astype(F32)).astype(BF16)


def dot(a, b):
    return jnp.dot(a, b, preferred_element_type=F32)


def dot_nt(a, b):
    return lax.dot_general(a, b, MAT_NT, preferred_element_type=F32)


def pad_rows(value, rows):
    return jnp.concatenate(
        [value, jnp.zeros((rows - value.shape[0], value.shape[1]), value.dtype)], axis=0
    )


def parity_at(index):
    degree = jnp.zeros_like(index)
    for step in range(1, ORDER + 1):
        degree = degree + (index >= step * step).astype(jnp.int32)
    return (1 - 2 * (degree & 1)).astype(F32)


def peer_offset(slot, reach):
    return slot - reach if slot < reach else slot - reach + 1


def stacked(value, coeffs):
    head = coeffs - 1
    high = value.astype(BF16).astype(F32)
    low = value - high
    row = lax.broadcasted_iota(jnp.int32, (2 * LANES - 3 * head, value.shape[1]), 0)
    last = jnp.where(row == 1, low[head:], jnp.where(row < 3, high[head:], 0.0))
    return jnp.concatenate([high[:head], low[:head], high[:head], last], axis=0)


def tagged(value, coeffs):
    head = coeffs - 1
    last = value[head : head + 1]
    row = lax.broadcasted_iota(jnp.int32, (LANES - head, value.shape[1]), 0)
    low = last - last.astype(BF16).astype(F32)
    tail = jnp.where(row == 1, low, jnp.where(row < 3, last, 0.0))
    return jnp.concatenate([value[:head], tail], axis=0)


def paired(rows, coeffs):
    head = coeffs - 1
    high = rows.astype(BF16).astype(F32)
    low = pltpu.roll(rows - high, head, 1)
    again = pltpu.roll(high, 2 * head - LANES, 1)
    lane = lax.broadcasted_iota(jnp.int32, rows.shape, 1)
    left = jnp.where(lane < head, high, low)
    right = jnp.where(lane < 2 * head - LANES, low, again)
    return jnp.concatenate([left, right], axis=1).astype(BF16)


def halo_out(rows, coeffs):
    lane = lax.broadcasted_iota(jnp.int32, (1, LANES), 1)
    room = LANES - coeffs
    last = rows[HALO - 1 :]
    first = jnp.where(lane < coeffs, rows[:1], pltpu.roll(last, coeffs, 1))
    second = jnp.where(lane < coeffs, rows[1:2], pltpu.roll(last, coeffs - room, 1))
    return jnp.concatenate([first, second, rows[2 : HALO - 1]], axis=0)


def halo_in(sent, coeffs):
    lane = lax.broadcasted_iota(jnp.int32, (1, LANES), 1)
    room = LANES - coeffs
    last = jnp.where(
        lane < room, pltpu.roll(sent[:1], room, 1), pltpu.roll(sent[1:2], LANES + room - coeffs, 1)
    )
    rows = jnp.concatenate([sent, last], axis=0)
    return jnp.where(lax.broadcasted_iota(jnp.int32, rows.shape, 1) < coeffs, rows, 0.0)


def peer_of(me, slot, reach, devices):
    other = me[0] + peer_offset(slot, reach)
    there = jnp.logical_and(other >= 0, other < devices)
    return jnp.where(there, other, me[0]), there


def export_kernel(me, devices, reach, x_ref, idx_ref, par_ref, out_ref):
    coeffs, cells = x_ref.shape
    rows = -(-coeffs // 8) * 8
    both = jnp.concatenate(split(pad_rows(x_ref[...], rows)), axis=0)
    peers = idx_ref.shape[0]
    room = jnp.zeros((HALO, LANES - coeffs), F32)
    line = lax.broadcasted_iota(jnp.int32, (cells, LANES), 0)

    def hot(slot):
        return jnp.where(line == idx_ref[slot], 1.0, 0.0).astype(BF16)

    for slot in range(0, peers, 2):
        sent = dot(both, jnp.concatenate([hot(slot), hot(slot + 1)], axis=1))
        sent = sent[:rows] + sent[rows:]
        for k in range(2):
            other, _ = peer_of(me, slot + k, reach, devices)
            out_ref[other, :rows] = sent[:, k * LANES : (k + 1) * LANES]
    total = par_ref.shape[0]
    for slot, start in ((reach - 1, 0), (reach, total - HALO)):
        other, _ = peer_of(me, slot, reach, devices)
        parents = jnp.concatenate([par_ref[start : start + HALO, :], room], axis=1)
        out_ref[other, coeffs : coeffs + HALO - 1] = halo_out(parents, coeffs)


def ops_kernel(m2l_ref, out_ref, turned):
    coeffs = m2l_ref.shape[0]
    pitch = out_ref.shape[0] // LANES
    for i in range(coeffs):
        turned[pl.ds(i, pitch, pitch), :] = pad_rows(m2l_ref[i], pitch)
    for j in range(coeffs):
        block = pad_rows(turned[j * pitch : j * pitch + coeffs, :], LANES).T
        out_ref[pl.ds(j, LANES, pitch), :] = block
    out_ref[pl.ds(coeffs, LANES, pitch), :] = block
    out_ref[pl.ds(coeffs + 1, LANES, pitch), :] = block - block.astype(BF16).astype(F32)
    for j in range(coeffs + 2, pitch):
        out_ref[pl.ds(j, LANES, pitch), :] = jnp.zeros((LANES, LANES), F32)


def weights_of(w_ref, start, pitch, coeffs):
    head = coeffs - 1
    high, low = split(w_ref[pl.ds(start, head), :])
    last = pad_rows(w_ref[pl.ds(start + head, pitch - head), :], 2 * LANES - 3 * head).astype(BF16)
    return jnp.concatenate([high, high, low, last], axis=0)


def products(columns, w_ref, first, pitch, slots, coeffs):
    return jnp.concatenate(
        [
            dot(
                columns[k * slots : (k + 1) * slots],
                weights_of(w_ref, (first + k) * pitch, pitch, coeffs),
            )
            for k in range(GROUP // slots)
        ],
        axis=0,
    )


def source_kernel(devices, reach, steps_total, me, src, x_ref, tgt_ref, cnt_ref, w_ref, ret_ref, own_ref, table, lists, bufs, accs):
    step = pl.program_id(0)
    steps = pl.num_programs(0)
    coeffs, cells = x_ref.shape
    slots, classes = tgt_ref.shape
    block = classes // steps
    per = GROUP // slots
    groups = block // per
    pitch = w_ref.shape[0] // block

    @pl.when(step == 0)
    def _():
        sign = parity_at(lax.broadcasted_iota(jnp.int32, (coeffs, cells), 0))
        table[...] = stacked(x_ref[...] * sign, coeffs).T.astype(BF16)
        slot = lax.broadcasted_iota(jnp.int32, (slots, classes), 0)
        live = jnp.where(slot < cnt_ref[...], tgt_ref[...], -1)
        for k in range(steps_total):
            lists[k, :, :block] = live[:, k * block : (k + 1) * block]
        for acc in accs:
            acc[...] = jnp.zeros_like(acc)

    line = lax.broadcasted_iota(jnp.int32, (slots, cells), 1)
    listed = lists[step]

    def compute(g):
        hot = jnp.concatenate(
            [
                jnp.where(listed[:, k : k + 1] == line, 1.0, 0.0).astype(BF16)
                for k in range(g * per, (g + 1) * per)
            ],
            axis=0,
        )
        columns = dot(hot, table[...]).astype(BF16)
        bufs[g % 2][...] = products(columns, w_ref, g * per, pitch, slots, coeffs)

    def scatter(buf, base):
        for q in range(GROUP):
            acc = accs[q % len(accs)]
            row = src[q % slots, base + q // slots]
            acc[pl.ds(row, 1), :] += buf[q : q + 1, :]

    base = step * block
    compute(0)
    for g in range(1, groups):
        compute(g)
        scatter(bufs[(g - 1) % 2], base + (g - 1) * per)
    scatter(bufs[(groups - 1) % 2], base + (groups - 1) * per)

    @pl.when(step == steps - 1)
    def _():
        sign = parity_at(lax.broadcasted_iota(jnp.int32, (LANES, LANES), 1))

        def total(start):
            value = accs[0][start : start + LANES, :]
            for acc in accs[1:]:
                value = value + acc[start : start + LANES, :]
            return value * sign

        for start in range(0, cells, LANES):
            own_ref[start : start + LANES, :] = total(start)
        rows = ret_ref.shape[1]
        for slot in range((accs[0].shape[0] - cells) // LANES):
            other, _ = peer_of(me, slot, reach, devices)
            ret_ref[other] = total(cells + slot * LANES).T[:rows]


def target_kernel(
    devices, reach, slots, me, src, x_ref, got_ref, tgt_ref, w_ref, own_ref, par_ref, pos_ref, oct_ref, l2l_ref,
    out_ref, table, near, bufs,
):
    step = pl.program_id(0)
    steps = pl.num_programs(0)
    coeffs, cells = x_ref.shape
    groups = tgt_ref.shape[1]
    classes = GROUP // slots
    pitch = w_ref.shape[0] // (groups * classes)

    @pl.when(step == 0)
    def _():
        table[:cells, :] = tagged(x_ref[...], coeffs).T
        for slot in range((table.shape[0] - cells) // LANES):
            other, _ = peer_of(me, slot, reach, devices)
            start = cells + slot * LANES
            table[start : start + LANES, :] = tagged(got_ref[other, :coeffs], coeffs).T
        near[...] = jnp.zeros_like(near)

    line = lax.broadcasted_iota(jnp.int32, (cells, GROUP), 0)

    def gather(buf, base):
        for q in range(GROUP):
            buf[q : q + 1, :] = table[pl.ds(src[q % slots, base + q // slots], 1), :]

    def compute(g):
        y = products(paired(bufs[g % 2][...], coeffs), w_ref, g * classes, pitch, slots, coeffs)
        hot = jnp.where(tgt_ref[0, g : g + 1, :] == line, 1.0, 0.0).astype(BF16)
        near[...] += dot(hot, jnp.concatenate(split(y), axis=1))

    base = step * groups * classes
    gather(bufs[0], base)
    for g in range(groups):
        if g + 1 < groups:
            gather(bufs[(g + 1) % 2], base + (g + 1) * classes)
        compute(g)

    @pl.when(step == steps - 1)
    def _():
        room = jnp.zeros((par_ref.shape[0], LANES - coeffs), F32)
        parts = [None, jnp.concatenate([par_ref[...], room], axis=1), None]
        for part, shift in ((0, -1), (2, 1)):
            other = jnp.clip(me[0] + shift, 0, devices - 1)
            sent = halo_in(got_ref[other, coeffs : coeffs + HALO - 1], coeffs)
            parts[part] = jnp.where(other == me[0], 0.0, sent)
        parents = jnp.concatenate(parts, axis=0)
        wide = parents.shape[0]
        parents = jnp.concatenate(split(parents.T), axis=0)
        hot = jnp.where(
            pos_ref[...] == lax.broadcasted_iota(jnp.int32, (wide, cells), 0), 1.0, 0.0
        ).astype(BF16)
        picked = dot(parents, hot).astype(BF16)
        total = (near[:, :LANES] + near[:, LANES:] + own_ref[...]).T[:coeffs]
        for k in range(l2l_ref.shape[0]):
            high, low = split(l2l_ref[k])
            filler = jnp.zeros((coeffs, LANES - coeffs), BF16)
            rows = jnp.concatenate([high, filler, high, filler], axis=1)
            term = dot(rows, picked)
            rows = jnp.concatenate([low, filler], axis=1)
            term = term + dot(rows, picked[:LANES])
            total = total + jnp.where(oct_ref[...] == k, term, 0.0)
        out_ref[...] = total


def back_kernel(devices, reach, me, base_ref, got_ref, idx_ref, out_ref):
    coeffs, cells = base_ref.shape
    rows = got_ref.shape[1]
    line = lax.broadcasted_iota(jnp.int32, (cells, LANES), 0)
    total = jnp.zeros((2 * rows, cells), F32)
    for slot in range(0, idx_ref.shape[0], 2):
        hots, gots = [], []
        for k in (slot, slot + 1):
            other, there = peer_of(me, k, reach, devices)
            place = jnp.where(there, idx_ref[k], -1)
            hots.append(jnp.where(line == place, 1.0, 0.0).astype(BF16))
            gots.append(jnp.concatenate(split(got_ref[other]), axis=0))
        total = total + dot_nt(jnp.concatenate(gots, axis=1), jnp.concatenate(hots, axis=1))
    out_ref[...] = base_ref[...] + total[:coeffs] + total[rows : rows + coeffs]


def vmem():
    return pl.BlockSpec(memory_space=pltpu.VMEM)


def smem():
    return pl.BlockSpec(memory_space=pltpu.SMEM)


LIMIT = 56 * 1024 * 1024


def shards(
    multipoles, parent_locals, m2l_ops, l2l_ops, export_cells, pair_first, pair_second, pair_count, parent_of, octant
):
    axes = ("gx", "gy")
    coeffs, cells = multipoles.shape
    exported = jnp.transpose(export_cells, (1, 0, 2))
    peers, _, send = exported.shape
    parents = parent_locals.T
    reach = peers // 2
    classes = m2l_ops.shape[2]
    slots = pair_first.shape[2]
    devices = lax.axis_size("gx") * lax.axis_size("gy")
    position = lax.axis_index("gx") * lax.axis_size("gy") + lax.axis_index("gy")
    me = position.reshape(1).astype(jnp.int32)
    rows = -(-coeffs // 8) * 8
    steps = 4
    groups = classes * slots // (GROUP * steps)

    outgoing = pl.pallas_call(
        lambda me, *refs: export_kernel(me, devices, reach, *refs),
        out_shape=jax.ShapeDtypeStruct((devices, coeffs + HALO - 1, send), F32),
        in_specs=[smem(), vmem(), vmem(), vmem()],
        out_specs=vmem(),
        compiler_params=pltpu.CompilerParams(vmem_limit_bytes=LIMIT),
        cost_estimate=pl.CostEstimate(flops=10**9, bytes_accessed=2 * 10**6, transcendentals=0),
        name="exports",
    )(me, multipoles, exported, parents)
    arrived = lax.all_to_all(outgoing, axes, 0, 0, tiled=True)

    weights = pl.pallas_call(
        ops_kernel,
        out_shape=jax.ShapeDtypeStruct((classes * rows, LANES), F32),
        grid=(classes // LANES,),
        in_specs=[pl.BlockSpec((coeffs, coeffs, LANES), lambda s: (0, 0, s))],
        out_specs=pl.BlockSpec((LANES * rows, LANES), lambda s: (s, 0)),
        scratch_shapes=[pltpu.VMEM((rows * rows, LANES), F32)],
        compiler_params=pltpu.CompilerParams(vmem_limit_bytes=LIMIT),
        cost_estimate=pl.CostEstimate(flops=10**9, bytes_accessed=20 * 10**6, transcendentals=0),
        name="operators",
    )(m2l_ops)

    source = pair_second[0].T
    w_spec = pl.BlockSpec((groups * GROUP // slots * rows, LANES), lambda s, *_: (s, 0))
    whole = pl.BlockSpec(memory_space=pltpu.VMEM)
    returned, own = pl.pallas_call(
        lambda me, src, x, t, n, w, r, o, table, lists, b0, b1, *accs: source_kernel(
            devices, reach, steps, me, src, x, t, n, w, r, o, table, lists, (b0, b1), accs
        ),
        out_shape=(
            jax.ShapeDtypeStruct((devices, rows, send), F32),
            jax.ShapeDtypeStruct((cells, LANES), F32),
        ),
        grid_spec=pltpu.PrefetchScalarGridSpec(
            num_scalar_prefetch=2,
            grid=(steps,),
            in_specs=[whole, whole, whole, w_spec],
            out_specs=(whole, whole),
            scratch_shapes=[
                pltpu.VMEM((cells, 2 * LANES), BF16),
                pltpu.VMEM((steps, slots, -(-classes // steps // LANES) * LANES), jnp.int32),
                pltpu.VMEM((GROUP, LANES), F32),
                pltpu.VMEM((GROUP, LANES), F32),
            ]
            + [pltpu.VMEM((cells + peers * send, LANES), F32)] * ACCS,
        ),
        compiler_params=pltpu.CompilerParams(vmem_limit_bytes=LIMIT),
        cost_estimate=pl.CostEstimate(flops=20 * 10**9, bytes_accessed=50 * 10**6, transcendentals=0),
        name="to_source",
    )(me, source, multipoles, pair_first[0].T, pair_count, weights)
    back = lax.all_to_all(returned, axes, 0, 0, tiled=True)

    own, pair_first, pair_count = lax.optimization_barrier((own, pair_first, pair_count))
    live = lax.broadcasted_iota(jnp.int32, (classes, slots), 1) < pair_count[0][:, None]
    target_rows = jnp.where(live, pair_first[0], -1).reshape(steps, groups, GROUP)
    place = (parent_of - position * parent_locals.shape[1] + HALO).reshape(1, cells)
    base = pl.pallas_call(
        lambda *refs: target_kernel(devices, reach, slots, *refs[:14], refs[14:]),
        out_shape=jax.ShapeDtypeStruct((coeffs, cells), F32),
        grid_spec=pltpu.PrefetchScalarGridSpec(
            num_scalar_prefetch=2,
            grid=(steps,),
            in_specs=[whole, whole, pl.BlockSpec((1, groups, GROUP), lambda s, *_: (s, 0, 0)), w_spec]
            + [whole] * 5,
            out_specs=whole,
            scratch_shapes=[
                pltpu.VMEM((cells + peers * send, LANES), F32),
                pltpu.VMEM((cells, 2 * LANES), F32),
                pltpu.VMEM((GROUP, LANES), F32),
                pltpu.VMEM((GROUP, LANES), F32),
            ],
        ),
        compiler_params=pltpu.CompilerParams(vmem_limit_bytes=LIMIT),
        cost_estimate=pl.CostEstimate(flops=20 * 10**9, bytes_accessed=50 * 10**6, transcendentals=0),
        name="to_target",
    )(me, source, multipoles, arrived, target_rows, weights, own, parents, place, octant.reshape(1, cells), l2l_ops)

    return pl.pallas_call(
        lambda me, *refs: back_kernel(devices, reach, me, *refs),
        out_shape=jax.ShapeDtypeStruct((coeffs, cells), F32),
        in_specs=[smem(), vmem(), vmem(), vmem()],
        out_specs=vmem(),
        compiler_params=pltpu.CompilerParams(vmem_limit_bytes=LIMIT // 4),
        cost_estimate=pl.CostEstimate(flops=10**9, bytes_accessed=2 * 10**6, transcendentals=0),
        name="returned",
    )(me, base, back, exported)


def solution(mesh):
    placed = (
        P(None, ("gx", "gy")),
        P(None, ("gx", "gy")),
        P(),
        P(),
        P(("gx", "gy"), None, None),
        P(("gx", "gy"), None, None),
        P(("gx", "gy"), None, None),
        P(("gx", "gy"), None),
        P(("gx", "gy")),
        P(("gx", "gy")),
    )
    return jax.shard_map(
        shards, mesh=mesh, in_specs=placed, out_specs=P(None, ("gx", "gy")), check_vma=False
    )
```

```python
import jax
import jax.numpy as jnp
from jax import lax
from jax.experimental import pallas as pl
from jax.experimental.pallas import tpu as pltpu
from jax.sharding import PartitionSpec as P

ORDER = 8
HALO = 16
LANES = 128
GROUP = 256
ACCS = 8
F32 = jnp.float32
BF16 = jnp.bfloat16
MAT_NT = (((1,), (1,)), ((), ()))


def split(value):
    high = value.astype(BF16)
    return high, (value - high.astype(F32)).astype(BF16)


def dot(a, b):
    return jnp.dot(a, b, preferred_element_type=F32)


def dot_nt(a, b):
    return lax.dot_general(a, b, MAT_NT, preferred_element_type=F32)


def pad_rows(value, rows):
    return jnp.concatenate(
        [value, jnp.zeros((rows - value.shape[0], value.shape[1]), value.dtype)], axis=0
    )


def parity_at(index):
    degree = jnp.zeros_like(index)
    for step in range(1, ORDER + 1):
        degree = degree + (index >= step * step).astype(jnp.int32)
    return (1 - 2 * (degree & 1)).astype(F32)


def peer_offset(slot, reach):
    return slot - reach if slot < reach else slot - reach + 1


def stacked(value, coeffs):
    head = coeffs - 1
    high = value.astype(BF16).astype(F32)
    low = value - high
    row = lax.broadcasted_iota(jnp.int32, (2 * LANES - 3 * head, value.shape[1]), 0)
    last = jnp.where(row == 1, low[head:], jnp.where(row < 3, high[head:], 0.0))
    return jnp.concatenate([high[:head], low[:head], high[:head], last], axis=0)


def tagged(value, coeffs):
    head = coeffs - 1
    last = value[head : head + 1]
    row = lax.broadcasted_iota(jnp.int32, (LANES - head, value.shape[1]), 0)
    low = last - last.astype(BF16).astype(F32)
    tail = jnp.where(row == 1, low, jnp.where(row < 3, last, 0.0))
    return jnp.concatenate([value[:head], tail], axis=0)


def paired(rows, coeffs):
    head = coeffs - 1
    high = rows.astype(BF16).astype(F32)
    low = pltpu.roll(rows - high, head, 1)
    again = pltpu.roll(high, 2 * head - LANES, 1)
    lane = lax.broadcasted_iota(jnp.int32, rows.shape, 1)
    left = jnp.where(lane < head, high, low)
    right = jnp.where(lane < 2 * head - LANES, low, again)
    return jnp.concatenate([left, right], axis=1).astype(BF16)


def halo_rows(coeffs):
    return -(-HALO * coeffs // LANES)


def halo_out(rows, coeffs):
    lane = lax.broadcasted_iota(jnp.int32, (1, LANES), 1)
    room, kept = LANES - coeffs, halo_rows(coeffs)
    spare = []
    for k in range(kept, HALO):
        for start in range(0, coeffs, room):
            spare.append(pltpu.roll(rows[k : k + 1], (coeffs - start) % LANES, 1))
    spare += [jnp.zeros((1, LANES), F32)] * (kept - len(spare))
    spare = jnp.concatenate(spare, axis=0)
    return jnp.where(lane < coeffs, rows[:kept], spare)


def halo_in(sent, coeffs):
    lane = lax.broadcasted_iota(jnp.int32, (1, LANES), 1)
    room, kept = LANES - coeffs, halo_rows(coeffs)
    rows, at = [sent], 0
    for k in range(kept, HALO):
        row = jnp.zeros((1, LANES), F32)
        for start in range(0, coeffs, room):
            piece = pltpu.roll(sent[at : at + 1], (start - coeffs) % LANES, 1)
            row = jnp.where(jnp.logical_and(lane >= start, lane < start + room), piece, row)
            at += 1
        rows.append(row)
    rows = jnp.concatenate(rows, axis=0)
    return jnp.where(lax.broadcasted_iota(jnp.int32, rows.shape, 1) < coeffs, rows, 0.0)


def peer_of(me, slot, reach, devices):
    other = me[0] + peer_offset(slot, reach)
    there = jnp.logical_and(other >= 0, other < devices)
    return jnp.where(there, other, me[0]), there


def export_kernel(me, devices, reach, x_ref, idx_ref, par_ref, out_ref):
    coeffs, cells = x_ref.shape
    rows = -(-coeffs // 8) * 8
    both = jnp.concatenate(split(pad_rows(x_ref[...], rows)), axis=0)
    peers = idx_ref.shape[0]
    held = out_ref.shape[0] // devices
    room = jnp.zeros((HALO, LANES - coeffs), F32)
    line = lax.broadcasted_iota(jnp.int32, (cells, LANES), 0)

    def hot(slot):
        return jnp.where(line == idx_ref[slot], 1.0, 0.0).astype(BF16)

    for slot in range(0, peers, 2):
        sent = dot(both, jnp.concatenate([hot(slot), hot(slot + 1)], axis=1))
        sent = sent[:rows] + sent[rows:]
        for k in range(2):
            other, _ = peer_of(me, slot + k, reach, devices)
            out_ref[pl.ds(other * held, coeffs), :] = sent[:coeffs, k * LANES : (k + 1) * LANES]
    total = par_ref.shape[0]
    for slot, start in ((reach - 1, 0), (reach, total - HALO)):
        other, _ = peer_of(me, slot, reach, devices)
        parents = jnp.concatenate([par_ref[start : start + HALO, :], room], axis=1)
        out_ref[pl.ds(other * held + coeffs, held - coeffs), :] = halo_out(parents, coeffs)


def ops_kernel(m2l_ref, out_ref, turned):
    coeffs = m2l_ref.shape[0]
    pitch = out_ref.shape[0] // LANES
    for i in range(coeffs):
        turned[pl.ds(i, pitch, pitch), :] = pad_rows(m2l_ref[i], pitch)
    for j in range(coeffs):
        block = pad_rows(turned[j * pitch : j * pitch + coeffs, :], LANES).T
        out_ref[pl.ds(j, LANES, pitch), :] = block
    out_ref[pl.ds(coeffs, LANES, pitch), :] = block
    out_ref[pl.ds(coeffs + 1, LANES, pitch), :] = block - block.astype(BF16).astype(F32)
    for j in range(coeffs + 2, pitch):
        out_ref[pl.ds(j, LANES, pitch), :] = jnp.zeros((LANES, LANES), F32)


def weights_of(w_ref, start, pitch, coeffs):
    head = coeffs - 1
    high, low = split(w_ref[pl.ds(start, head), :])
    last = pad_rows(w_ref[pl.ds(start + head, pitch - head), :], 2 * LANES - 3 * head).astype(BF16)
    return jnp.concatenate([high, high, low, last], axis=0)


def products(columns, w_ref, first, pitch, slots, coeffs):
    return jnp.concatenate(
        [
            dot(
                columns[k * slots : (k + 1) * slots],
                weights_of(w_ref, (first + k) * pitch, pitch, coeffs),
            )
            for k in range(GROUP // slots)
        ],
        axis=0,
    )


def source_kernel(devices, reach, steps_total, me, src, x_ref, tgt_ref, cnt_ref, w_ref, ret_ref, own_ref, live_ref, table, lists, bufs, accs):
    step = pl.program_id(0)
    steps = pl.num_programs(0)
    coeffs, cells = x_ref.shape
    slots, classes = tgt_ref.shape
    block = classes // steps
    per = GROUP // slots
    groups = block // per
    pitch = w_ref.shape[0] // block

    @pl.when(step == 0)
    def _():
        sign = parity_at(lax.broadcasted_iota(jnp.int32, (coeffs, cells), 0))
        table[...] = stacked(x_ref[...] * sign, coeffs).T.astype(BF16)
        slot = lax.broadcasted_iota(jnp.int32, (slots, classes), 0)
        live = jnp.where(slot < cnt_ref[...], tgt_ref[...], -1)
        live_ref[...] = live.T
        for k in range(steps_total):
            lists[k, :, :block] = live[:, k * block : (k + 1) * block]
        for acc in accs:
            acc[...] = jnp.zeros_like(acc)

    line = lax.broadcasted_iota(jnp.int32, (slots, cells), 1)
    listed = lists[step]

    def compute(g):
        hot = jnp.concatenate(
            [
                jnp.where(listed[:, k : k + 1] == line, 1.0, 0.0).astype(BF16)
                for k in range(g * per, (g + 1) * per)
            ],
            axis=0,
        )
        columns = dot(hot, table[...]).astype(BF16)
        bufs[g % 2][...] = products(columns, w_ref, g * per, pitch, slots, coeffs)

    def scatter(buf, base):
        for q in range(GROUP):
            acc = accs[q % len(accs)]
            row = src[q % slots, base + q // slots]
            acc[pl.ds(row, 1), :] += buf[q : q + 1, :]

    base = step * block
    compute(0)
    for g in range(1, groups):
        compute(g)
        scatter(bufs[(g - 1) % 2], base + (g - 1) * per)
    scatter(bufs[(groups - 1) % 2], base + (groups - 1) * per)

    @pl.when(step == steps - 1)
    def _():
        sign = parity_at(lax.broadcasted_iota(jnp.int32, (LANES, LANES), 1))

        def total(start):
            value = accs[0][start : start + LANES, :]
            for acc in accs[1:]:
                value = value + acc[start : start + LANES, :]
            return value * sign

        for start in range(0, cells, LANES):
            own_ref[start : start + LANES, :] = total(start)
        for slot in range((accs[0].shape[0] - cells) // LANES):
            other, _ = peer_of(me, slot, reach, devices)
            ret_ref[pl.ds(other * coeffs, coeffs), :] = total(cells + slot * LANES).T[:coeffs]


def target_kernel(
    devices, reach, slots, me, src, x_ref, got_ref, tgt_ref, w_ref, own_ref, par_ref, pos_ref, oct_ref, l2l_ref,
    out_ref, table, near, bufs,
):
    step = pl.program_id(0)
    steps = pl.num_programs(0)
    coeffs, cells = x_ref.shape
    held = got_ref.shape[0] // devices
    groups = tgt_ref.shape[1]
    classes = GROUP // slots
    pitch = w_ref.shape[0] // (groups * classes)

    @pl.when(step == 0)
    def _():
        table[:cells, :] = tagged(x_ref[...], coeffs).T
        for slot in range((table.shape[0] - cells) // LANES):
            other, _ = peer_of(me, slot, reach, devices)
            start = cells + slot * LANES
            table[start : start + LANES, :] = tagged(got_ref[pl.ds(other * held, coeffs), :], coeffs).T
        near[...] = jnp.zeros_like(near)

    line = lax.broadcasted_iota(jnp.int32, (cells, GROUP), 0)

    def gather(buf, base):
        for q in range(GROUP):
            buf[q : q + 1, :] = table[pl.ds(src[q % slots, base + q // slots], 1), :]

    def compute(g):
        y = products(paired(bufs[g % 2][...], coeffs), w_ref, g * classes, pitch, slots, coeffs)
        hot = jnp.where(tgt_ref[0, g : g + 1, :] == line, 1.0, 0.0).astype(BF16)
        near[...] += dot(hot, jnp.concatenate(split(y), axis=1))

    base = step * groups * classes
    gather(bufs[0], base)
    for g in range(groups):
        if g + 1 < groups:
            gather(bufs[(g + 1) % 2], base + (g + 1) * classes)
        compute(g)

    @pl.when(step == steps - 1)
    def _():
        room = jnp.zeros((par_ref.shape[0], LANES - coeffs), F32)
        parts = [None, jnp.concatenate([par_ref[...], room], axis=1), None]
        for part, shift in ((0, -1), (2, 1)):
            other = jnp.clip(me[0] + shift, 0, devices - 1)
            sent = halo_in(got_ref[pl.ds(other * held + coeffs, held - coeffs), :], coeffs)
            parts[part] = jnp.where(other == me[0], 0.0, sent)
        parents = jnp.concatenate(parts, axis=0)
        wide = parents.shape[0]
        parents = jnp.concatenate(split(parents.T), axis=0)
        hot = jnp.where(
            pos_ref[...] - (me[0] * par_ref.shape[0] - HALO) == lax.broadcasted_iota(jnp.int32, (wide, cells), 0), 1.0, 0.0
        ).astype(BF16)
        picked = dot(parents, hot).astype(BF16)
        total = (near[:, :LANES] + near[:, LANES:] + own_ref[...]).T[:coeffs]
        for k in range(l2l_ref.shape[0]):
            high, low = split(l2l_ref[k])
            filler = jnp.zeros((coeffs, LANES - coeffs), BF16)
            rows = jnp.concatenate([high, filler, high, filler], axis=1)
            term = dot(rows, picked)
            rows = jnp.concatenate([low, filler], axis=1)
            term = term + dot(rows, picked[:LANES])
            total = total + jnp.where(oct_ref[...] == k, term, 0.0)
        out_ref[...] = total


def back_kernel(devices, reach, me, base_ref, got_any, idx_ref, out_ref, got_ref, done):
    coeffs, cells = base_ref.shape
    rows = -(-coeffs // 8) * 8
    copy = pltpu.make_async_copy(got_any, got_ref, done)
    copy.start()
    line = lax.broadcasted_iota(jnp.int32, (cells, LANES), 0)
    total = jnp.zeros((2 * rows, cells), F32)
    copy.wait()
    for slot in range(0, idx_ref.shape[0], 2):
        hots, gots = [], []
        for k in (slot, slot + 1):
            other, there = peer_of(me, k, reach, devices)
            place = jnp.where(there, idx_ref[k], -1)
            hots.append(jnp.where(line == place, 1.0, 0.0).astype(BF16))
            got = pad_rows(got_ref[pl.ds(other * coeffs, coeffs), :], rows)
            gots.append(jnp.concatenate(split(got), axis=0))
        total = total + dot_nt(jnp.concatenate(gots, axis=1), jnp.concatenate(hots, axis=1))
    out_ref[...] = base_ref[...] + total[:coeffs] + total[rows : rows + coeffs]


def vmem():
    return pl.BlockSpec(memory_space=pltpu.VMEM)


def smem():
    return pl.BlockSpec(memory_space=pltpu.SMEM)


LIMIT = 56 * 1024 * 1024


def shards(
    multipoles, parent_locals, m2l_ops, l2l_ops, export_cells, pair_first, pair_second, pair_count, parent_of, octant
):
    axes = ("gx", "gy")
    coeffs, cells = multipoles.shape
    exported = jnp.transpose(export_cells, (1, 0, 2))
    peers, _, send = exported.shape
    parents = parent_locals.T
    reach = peers // 2
    classes = m2l_ops.shape[2]
    slots = pair_first.shape[2]
    devices = lax.axis_size("gx") * lax.axis_size("gy")
    position = lax.axis_index("gx") * lax.axis_size("gy") + lax.axis_index("gy")
    me = position.reshape(1).astype(jnp.int32)
    rows = -(-coeffs // 8) * 8
    steps = 4
    groups = classes * slots // (GROUP * steps)

    held = coeffs + halo_rows(coeffs)

    def exchange(blocks):
        lines = blocks.shape[0] // devices
        cut = blocks.reshape(devices, lines, 1, send)
        return lax.all_to_all(cut, axes, 0, 0, tiled=True).reshape(blocks.shape)

    outgoing = pl.pallas_call(
        lambda me, *refs: export_kernel(me, devices, reach, *refs),
        out_shape=jax.ShapeDtypeStruct((devices * held, send), F32),
        in_specs=[smem(), vmem(), vmem(), vmem()],
        out_specs=vmem(),
        compiler_params=pltpu.CompilerParams(vmem_limit_bytes=LIMIT),
        cost_estimate=pl.CostEstimate(flops=10**9, bytes_accessed=2 * 10**6, transcendentals=0),
        name="exports",
    )(me, multipoles, exported, parents)
    arrived = exchange(outgoing)

    weights = pl.pallas_call(
        ops_kernel,
        out_shape=jax.ShapeDtypeStruct((classes * rows, LANES), F32),
        grid=(classes // LANES,),
        in_specs=[pl.BlockSpec((coeffs, coeffs, LANES), lambda s: (0, 0, s))],
        out_specs=pl.BlockSpec((LANES * rows, LANES), lambda s: (s, 0)),
        scratch_shapes=[pltpu.VMEM((rows * rows, LANES), F32)],
        compiler_params=pltpu.CompilerParams(vmem_limit_bytes=LIMIT),
        cost_estimate=pl.CostEstimate(flops=10**9, bytes_accessed=20 * 10**6, transcendentals=0),
        name="operators",
    )(m2l_ops)

    source = pair_second[0].T
    w_spec = pl.BlockSpec((groups * GROUP // slots * rows, LANES), lambda s, *_: (s, 0))
    whole = pl.BlockSpec(memory_space=pltpu.VMEM)
    returned, own, live = pl.pallas_call(
        lambda me, src, x, t, n, w, r, o, v, table, lists, b0, b1, *accs: source_kernel(
            devices, reach, steps, me, src, x, t, n, w, r, o, v, table, lists, (b0, b1), accs
        ),
        out_shape=(
            jax.ShapeDtypeStruct((devices * coeffs, send), F32),
            jax.ShapeDtypeStruct((cells, LANES), F32),
            jax.ShapeDtypeStruct((classes, slots), jnp.int32),
        ),
        grid_spec=pltpu.PrefetchScalarGridSpec(
            num_scalar_prefetch=2,
            grid=(steps,),
            in_specs=[whole, whole, whole, w_spec],
            out_specs=(whole, whole, whole),
            scratch_shapes=[
                pltpu.VMEM((cells, 2 * LANES), BF16),
                pltpu.VMEM((steps, slots, -(-classes // steps // LANES) * LANES), jnp.int32),
                pltpu.VMEM((GROUP, LANES), F32),
                pltpu.VMEM((GROUP, LANES), F32),
            ]
            + [pltpu.VMEM((cells + peers * send, LANES), F32)] * ACCS,
        ),
        compiler_params=pltpu.CompilerParams(vmem_limit_bytes=LIMIT),
        cost_estimate=pl.CostEstimate(flops=20 * 10**9, bytes_accessed=50 * 10**6, transcendentals=0),
        name="to_source",
    )(me, source, multipoles, pair_first[0].T, pair_count, weights)
    back = exchange(returned)

    target_rows = live.reshape(steps, groups, GROUP)
    base = pl.pallas_call(
        lambda *refs: target_kernel(devices, reach, slots, *refs[:14], refs[14:]),
        out_shape=jax.ShapeDtypeStruct((coeffs, cells), F32),
        grid_spec=pltpu.PrefetchScalarGridSpec(
            num_scalar_prefetch=2,
            grid=(steps,),
            in_specs=[whole, whole, pl.BlockSpec((1, groups, GROUP), lambda s, *_: (s, 0, 0)), w_spec]
            + [whole] * 5,
            out_specs=whole,
            scratch_shapes=[
                pltpu.VMEM((cells + peers * send, LANES), F32),
                pltpu.VMEM((cells, 2 * LANES), F32),
                pltpu.VMEM((GROUP, LANES), F32),
                pltpu.VMEM((GROUP, LANES), F32),
            ],
        ),
        compiler_params=pltpu.CompilerParams(vmem_limit_bytes=LIMIT),
        cost_estimate=pl.CostEstimate(flops=20 * 10**9, bytes_accessed=50 * 10**6, transcendentals=0),
        name="to_target",
    )(me, source, multipoles, arrived, target_rows, weights, own, parents, parent_of.reshape(1, cells), octant.reshape(1, cells), l2l_ops)

    return pl.pallas_call(
        lambda me, *refs: back_kernel(devices, reach, me, *refs),
        out_shape=jax.ShapeDtypeStruct((coeffs, cells), F32),
        in_specs=[smem(), vmem(), pl.BlockSpec(memory_space=pl.ANY), vmem()],
        out_specs=vmem(),
        scratch_shapes=[pltpu.VMEM(back.shape, F32), pltpu.SemaphoreType.DMA],
        compiler_params=pltpu.CompilerParams(vmem_limit_bytes=LIMIT // 4),
        cost_estimate=pl.CostEstimate(flops=10**9, bytes_accessed=2 * 10**6, transcendentals=0),
        name="returned",
    )(me, base, back, exported)


def solution(mesh):
    placed = (
        P(None, ("gx", "gy")),
        P(None, ("gx", "gy")),
        P(),
        P(),
        P(("gx", "gy"), None, None),
        P(("gx", "gy"), None, None),
        P(("gx", "gy"), None, None),
        P(("gx", "gy"), None),
        P(("gx", "gy")),
        P(("gx", "gy")),
    )
    return jax.shard_map(
        shards, mesh=mesh, in_specs=placed, out_specs=P(None, ("gx", "gy")), check_vma=False
    )
```

```python
import jax
import jax.numpy as jnp
from jax import lax
from jax.experimental import pallas as pl
from jax.experimental.pallas import tpu as pltpu
from jax.sharding import PartitionSpec as P

ORDER = 8
HALO = 16
LANES = 128
GROUP = 256
ACCS = 8
F32 = jnp.float32
BF16 = jnp.bfloat16
MAT_NT = (((1,), (1,)), ((), ()))


def split(value):
    high = value.astype(BF16)
    return high, (value - high.astype(F32)).astype(BF16)


def dot(a, b):
    return jnp.dot(a, b, preferred_element_type=F32)


def dot_nt(a, b):
    return lax.dot_general(a, b, MAT_NT, preferred_element_type=F32)


def pad_rows(value, rows):
    return jnp.concatenate(
        [value, jnp.zeros((rows - value.shape[0], value.shape[1]), value.dtype)], axis=0
    )


def parity_at(index):
    degree = jnp.zeros_like(index)
    for step in range(1, ORDER + 1):
        degree = degree + (index >= step * step).astype(jnp.int32)
    return (1 - 2 * (degree & 1)).astype(F32)


def peer_offset(slot, reach):
    return slot - reach if slot < reach else slot - reach + 1


def stacked(value, coeffs):
    head = coeffs - 1
    high = value.astype(BF16).astype(F32)
    low = value - high
    row = lax.broadcasted_iota(jnp.int32, (2 * LANES - 3 * head, value.shape[1]), 0)
    last = jnp.where(row == 1, low[head:], jnp.where(row < 3, high[head:], 0.0))
    return jnp.concatenate([high[:head], low[:head], high[:head], last], axis=0)


def tagged(value, coeffs):
    head = coeffs - 1
    last = value[head : head + 1]
    row = lax.broadcasted_iota(jnp.int32, (LANES - head, value.shape[1]), 0)
    low = last - last.astype(BF16).astype(F32)
    tail = jnp.where(row == 1, low, jnp.where(row < 3, last, 0.0))
    return jnp.concatenate([value[:head], tail], axis=0)


def paired(rows, coeffs):
    head = coeffs - 1
    high = rows.astype(BF16).astype(F32)
    low = pltpu.roll(rows - high, head, 1)
    again = pltpu.roll(high, 2 * head - LANES, 1)
    lane = lax.broadcasted_iota(jnp.int32, rows.shape, 1)
    left = jnp.where(lane < head, high, low)
    right = jnp.where(lane < 2 * head - LANES, low, again)
    return jnp.concatenate([left, right], axis=1).astype(BF16)


def halo_rows(coeffs):
    return -(-HALO * coeffs // LANES)


def halo_out(rows, coeffs):
    lane = lax.broadcasted_iota(jnp.int32, (1, LANES), 1)
    room, kept = LANES - coeffs, halo_rows(coeffs)
    spare = []
    for k in range(kept, HALO):
        for start in range(0, coeffs, room):
            spare.append(pltpu.roll(rows[k : k + 1], (coeffs - start) % LANES, 1))
    spare += [jnp.zeros((1, LANES), F32)] * (kept - len(spare))
    spare = jnp.concatenate(spare, axis=0)
    return jnp.where(lane < coeffs, rows[:kept], spare)


def halo_in(sent, coeffs):
    lane = lax.broadcasted_iota(jnp.int32, (1, LANES), 1)
    room, kept = LANES - coeffs, halo_rows(coeffs)
    rows, at = [sent], 0
    for k in range(kept, HALO):
        row = jnp.zeros((1, LANES), F32)
        for start in range(0, coeffs, room):
            piece = pltpu.roll(sent[at : at + 1], (start - coeffs) % LANES, 1)
            row = jnp.where(jnp.logical_and(lane >= start, lane < start + room), piece, row)
            at += 1
        rows.append(row)
    rows = jnp.concatenate(rows, axis=0)
    return jnp.where(lax.broadcasted_iota(jnp.int32, rows.shape, 1) < coeffs, rows, 0.0)


def peer_of(me, slot, reach, devices):
    other = me[0] + peer_offset(slot, reach)
    there = jnp.logical_and(other >= 0, other < devices)
    return jnp.where(there, other, me[0]), there


def export_kernel(me, devices, reach, x_ref, idx_ref, par_ref, out_ref):
    coeffs, cells = x_ref.shape
    rows = -(-coeffs // 8) * 8
    both = jnp.concatenate(split(pad_rows(x_ref[...], rows)), axis=0)
    peers = idx_ref.shape[0]
    held = out_ref.shape[0] // devices
    room = jnp.zeros((HALO, LANES - coeffs), F32)
    line = lax.broadcasted_iota(jnp.int32, (cells, LANES), 0)

    def hot(slot):
        return jnp.where(line == idx_ref[slot], 1.0, 0.0).astype(BF16)

    for slot in range(0, peers, 2):
        sent = dot(both, jnp.concatenate([hot(slot), hot(slot + 1)], axis=1))
        sent = sent[:rows] + sent[rows:]
        for k in range(2):
            other, _ = peer_of(me, slot + k, reach, devices)
            out_ref[pl.ds(other * held, coeffs), :] = sent[:coeffs, k * LANES : (k + 1) * LANES]
    total = par_ref.shape[0]
    for slot, start in ((reach - 1, 0), (reach, total - HALO)):
        other, _ = peer_of(me, slot, reach, devices)
        parents = jnp.concatenate([par_ref[start : start + HALO, :], room], axis=1)
        out_ref[pl.ds(other * held + coeffs, held - coeffs), :] = halo_out(parents, coeffs)


def lay_out(m2l_ref, half, w_ref, turned):
    coeffs = m2l_ref.shape[0]
    pitch = w_ref.shape[1] // LANES
    for i in range(coeffs):
        turned[pl.ds(i, pitch, pitch), :] = pad_rows(m2l_ref[i], pitch)
    for j in range(coeffs):
        block = pad_rows(turned[j * pitch : j * pitch + coeffs, :], LANES).T
        w_ref[half, pl.ds(j, LANES, pitch), :] = block
    w_ref[half, pl.ds(coeffs, LANES, pitch), :] = block
    w_ref[half, pl.ds(coeffs + 1, LANES, pitch), :] = block - block.astype(BF16).astype(F32)
    for j in range(coeffs + 2, pitch):
        w_ref[half, pl.ds(j, LANES, pitch), :] = jnp.zeros((LANES, LANES), F32)


def weights_of(w_ref, start, pitch, coeffs):
    head = coeffs - 1
    high, low = split(w_ref[pl.ds(start, head), :])
    last = pad_rows(w_ref[pl.ds(start + head, pitch - head), :], 2 * LANES - 3 * head).astype(BF16)
    return jnp.concatenate([high, high, low, last], axis=0)


def products(columns, w_ref, first, pitch, slots, coeffs):
    return jnp.concatenate(
        [
            dot(
                columns[k * slots : (k + 1) * slots],
                weights_of(w_ref, (first + k) * pitch, pitch, coeffs),
            )
            for k in range(GROUP // slots)
        ],
        axis=0,
    )


def source_kernel(
    devices, reach, steps_total, me, src, x_ref, tgt_ref, cnt_ref, m2l_ref, ret_ref, own_ref, live_ref, w_any,
    table, lists, w_all, turned, sent, bufs, accs,
):
    step = pl.program_id(0)
    steps = pl.num_programs(0)
    coeffs, cells = x_ref.shape
    slots, classes = tgt_ref.shape
    block = classes // steps
    per = GROUP // slots
    groups = block // per
    pitch = w_all.shape[1] // LANES
    halves = w_all.shape[0]
    span = steps_total // halves
    half = step // span

    def copy_of(k):
        return pltpu.make_async_copy(w_all.at[k], w_any.at[k], sent.at[k])

    @pl.when(step % span == 0)
    def _():
        lay_out(m2l_ref, half, w_all, turned)
        copy_of(half).start()

    first = pl.multiple_of((step % span) * block * pitch, 8)
    w_ref = w_all.at[half, pl.ds(first, block * pitch), :]

    @pl.when(step == 0)
    def _():
        sign = parity_at(lax.broadcasted_iota(jnp.int32, (coeffs, cells), 0))
        table[...] = stacked(x_ref[...] * sign, coeffs).T.astype(BF16)
        slot = lax.broadcasted_iota(jnp.int32, (slots, classes), 0)
        live = jnp.where(slot < cnt_ref[...], tgt_ref[...], -1)
        live_ref[...] = live.T
        for k in range(steps_total):
            lists[k, :, :block] = live[:, k * block : (k + 1) * block]
        for acc in accs:
            acc[...] = jnp.zeros_like(acc)

    line = lax.broadcasted_iota(jnp.int32, (slots, cells), 1)
    listed = lists[step]

    def compute(g):
        hot = jnp.concatenate(
            [
                jnp.where(listed[:, k : k + 1] == line, 1.0, 0.0).astype(BF16)
                for k in range(g * per, (g + 1) * per)
            ],
            axis=0,
        )
        columns = dot(hot, table[...]).astype(BF16)
        bufs[g % 2][...] = products(columns, w_ref, g * per, pitch, slots, coeffs)

    def scatter(buf, base):
        for q in range(GROUP):
            acc = accs[q % len(accs)]
            row = src[q % slots, base + q // slots]
            acc[pl.ds(row, 1), :] += buf[q : q + 1, :]

    base = step * block
    compute(0)
    for g in range(1, groups):
        compute(g)
        scatter(bufs[(g - 1) % 2], base + (g - 1) * per)
    scatter(bufs[(groups - 1) % 2], base + (groups - 1) * per)

    @pl.when(step == steps - 1)
    def _():
        for k in range(halves):
            copy_of(k).wait()
        sign = parity_at(lax.broadcasted_iota(jnp.int32, (LANES, LANES), 1))

        def total(start):
            value = accs[0][start : start + LANES, :]
            for acc in accs[1:]:
                value = value + acc[start : start + LANES, :]
            return value * sign

        for start in range(0, cells, LANES):
            own_ref[start : start + LANES, :] = total(start)
        for slot in range((accs[0].shape[0] - cells) // LANES):
            other, _ = peer_of(me, slot, reach, devices)
            ret_ref[pl.ds(other * coeffs, coeffs), :] = total(cells + slot * LANES).T[:coeffs]


def target_kernel(
    devices, reach, slots, me, src, x_ref, got_ref, tgt_ref, w_ref, own_ref, par_ref, pos_ref, oct_ref, l2l_ref,
    out_ref, table, near, bufs,
):
    step = pl.program_id(0)
    steps = pl.num_programs(0)
    coeffs, cells = x_ref.shape
    held = got_ref.shape[0] // devices
    groups = tgt_ref.shape[1]
    classes = GROUP // slots
    pitch = w_ref.shape[0] // (groups * classes)

    @pl.when(step == 0)
    def _():
        table[:cells, :] = tagged(x_ref[...], coeffs).T
        for slot in range((table.shape[0] - cells) // LANES):
            other, _ = peer_of(me, slot, reach, devices)
            start = cells + slot * LANES
            table[start : start + LANES, :] = tagged(got_ref[pl.ds(other * held, coeffs), :], coeffs).T
        near[...] = jnp.zeros_like(near)

    line = lax.broadcasted_iota(jnp.int32, (cells, GROUP), 0)

    def gather(buf, base):
        for q in range(GROUP):
            buf[q : q + 1, :] = table[pl.ds(src[q % slots, base + q // slots], 1), :]

    def compute(g):
        y = products(paired(bufs[g % 2][...], coeffs), w_ref, g * classes, pitch, slots, coeffs)
        hot = jnp.where(tgt_ref[0, g : g + 1, :] == line, 1.0, 0.0).astype(BF16)
        near[...] += dot(hot, jnp.concatenate(split(y), axis=1))

    base = step * groups * classes
    gather(bufs[0], base)
    for g in range(groups):
        if g + 1 < groups:
            gather(bufs[(g + 1) % 2], base + (g + 1) * classes)
        compute(g)

    @pl.when(step == steps - 1)
    def _():
        room = jnp.zeros((par_ref.shape[0], LANES - coeffs), F32)
        parts = [None, jnp.concatenate([par_ref[...], room], axis=1), None]
        for part, shift in ((0, -1), (2, 1)):
            other = jnp.clip(me[0] + shift, 0, devices - 1)
            sent = halo_in(got_ref[pl.ds(other * held + coeffs, held - coeffs), :], coeffs)
            parts[part] = jnp.where(other == me[0], 0.0, sent)
        parents = jnp.concatenate(parts, axis=0)
        wide = parents.shape[0]
        parents = jnp.concatenate(split(parents.T), axis=0)
        hot = jnp.where(
            pos_ref[...] - (me[0] * par_ref.shape[0] - HALO) == lax.broadcasted_iota(jnp.int32, (wide, cells), 0), 1.0, 0.0
        ).astype(BF16)
        picked = dot(parents, hot).astype(BF16)
        total = (near[:, :LANES] + near[:, LANES:] + own_ref[...]).T[:coeffs]
        for k in range(l2l_ref.shape[0]):
            high, low = split(l2l_ref[k])
            filler = jnp.zeros((coeffs, LANES - coeffs), BF16)
            rows = jnp.concatenate([high, filler, high, filler], axis=1)
            term = dot(rows, picked)
            rows = jnp.concatenate([low, filler], axis=1)
            term = term + dot(rows, picked[:LANES])
            total = total + jnp.where(oct_ref[...] == k, term, 0.0)
        out_ref[...] = total


def back_kernel(devices, reach, me, base_ref, got_ref, idx_ref, out_ref):
    coeffs, cells = base_ref.shape
    rows = -(-coeffs // 8) * 8
    line = lax.broadcasted_iota(jnp.int32, (cells, LANES), 0)
    total = jnp.zeros((2 * rows, cells), F32)
    for slot in range(0, idx_ref.shape[0], 2):
        hots, gots = [], []
        for k in (slot, slot + 1):
            other, there = peer_of(me, k, reach, devices)
            place = jnp.where(there, idx_ref[k], -1)
            hots.append(jnp.where(line == place, 1.0, 0.0).astype(BF16))
            got = pad_rows(got_ref[pl.ds(other * coeffs, coeffs), :], rows)
            gots.append(jnp.concatenate(split(got), axis=0))
        total = total + dot_nt(jnp.concatenate(gots, axis=1), jnp.concatenate(hots, axis=1))
    out_ref[...] = base_ref[...] + total[:coeffs] + total[rows : rows + coeffs]


def vmem():
    return pl.BlockSpec(memory_space=pltpu.VMEM)


def smem():
    return pl.BlockSpec(memory_space=pltpu.SMEM)


LIMIT = 56 * 1024 * 1024


def shards(
    multipoles, parent_locals, m2l_ops, l2l_ops, export_cells, pair_first, pair_second, pair_count, parent_of, octant
):
    axes = ("gx", "gy")
    coeffs, cells = multipoles.shape
    exported = jnp.transpose(export_cells, (1, 0, 2))
    peers, _, send = exported.shape
    parents = parent_locals.T
    reach = peers // 2
    classes = m2l_ops.shape[2]
    slots = pair_first.shape[2]
    devices = lax.axis_size("gx") * lax.axis_size("gy")
    position = lax.axis_index("gx") * lax.axis_size("gy") + lax.axis_index("gy")
    me = position.reshape(1).astype(jnp.int32)
    rows = -(-coeffs // 8) * 8
    steps = 4
    groups = classes * slots // (GROUP * steps)

    held = coeffs + halo_rows(coeffs)

    def exchange(blocks):
        lines = blocks.shape[0] // devices
        cut = blocks.reshape(devices, lines, 1, send)
        return lax.all_to_all(cut, axes, 0, 0, tiled=True).reshape(blocks.shape)

    outgoing = pl.pallas_call(
        lambda me, *refs: export_kernel(me, devices, reach, *refs),
        out_shape=pltpu.VMEM((devices * held, send), F32),
        in_specs=[smem(), vmem(), vmem(), vmem()],
        out_specs=vmem(),
        compiler_params=pltpu.CompilerParams(vmem_limit_bytes=LIMIT),
        cost_estimate=pl.CostEstimate(flops=10**9, bytes_accessed=2 * 10**6, transcendentals=0),
        name="exports",
    )(me, multipoles, exported, parents)
    arrived = exchange(outgoing)

    source = pair_second[0].T
    w_spec = pl.BlockSpec((groups * GROUP // slots * rows, LANES), lambda s, *_: (s, 0))
    whole = pl.BlockSpec(memory_space=pltpu.VMEM)
    halves = classes // LANES
    span = steps // halves
    returned, own, live, weights = pl.pallas_call(
        lambda me, src, x, t, n, m, r, o, v, w, table, lists, wa, turned, sent, b0, b1, *accs: source_kernel(
            devices, reach, steps, me, src, x, t, n, m, r, o, v, w, table, lists, wa, turned, sent, (b0, b1), accs
        ),
        out_shape=(
            jax.ShapeDtypeStruct((devices * coeffs, send), F32),
            jax.ShapeDtypeStruct((cells, LANES), F32),
            jax.ShapeDtypeStruct((classes, slots), jnp.int32),
            jax.ShapeDtypeStruct((halves, LANES * rows, LANES), F32),
        ),
        grid_spec=pltpu.PrefetchScalarGridSpec(
            num_scalar_prefetch=2,
            grid=(steps,),
            in_specs=[whole, whole, whole, pl.BlockSpec((coeffs, coeffs, LANES), lambda s, *_: (0, 0, s // span))],
            out_specs=(whole, whole, whole, pl.BlockSpec(memory_space=pl.ANY)),
            scratch_shapes=[
                pltpu.VMEM((cells, 2 * LANES), BF16),
                pltpu.VMEM((steps, slots, -(-classes // steps // LANES) * LANES), jnp.int32),
                pltpu.VMEM((halves, LANES * rows, LANES), F32),
                pltpu.VMEM((rows * rows, LANES), F32),
                pltpu.SemaphoreType.DMA((halves,)),
                pltpu.VMEM((GROUP, LANES), F32),
                pltpu.VMEM((GROUP, LANES), F32),
            ]
            + [pltpu.VMEM((cells + peers * send, LANES), F32)] * ACCS,
        ),
        compiler_params=pltpu.CompilerParams(vmem_limit_bytes=LIMIT),
        cost_estimate=pl.CostEstimate(flops=20 * 10**9, bytes_accessed=50 * 10**6, transcendentals=0),
        name="to_source",
    )(me, source, multipoles, pair_first[0].T, pair_count, m2l_ops)
    weights = weights.reshape(classes * rows, LANES)
    back = pltpu.with_memory_space_constraint(exchange(returned), pltpu.VMEM)

    target_rows = live.reshape(steps, groups, GROUP)
    base = pl.pallas_call(
        lambda *refs: target_kernel(devices, reach, slots, *refs[:14], refs[14:]),
        out_shape=pltpu.VMEM((coeffs, cells), F32),
        grid_spec=pltpu.PrefetchScalarGridSpec(
            num_scalar_prefetch=2,
            grid=(steps,),
            in_specs=[whole, whole, pl.BlockSpec((1, groups, GROUP), lambda s, *_: (s, 0, 0)), w_spec]
            + [whole] * 5,
            out_specs=whole,
            scratch_shapes=[
                pltpu.VMEM((cells + peers * send, LANES), F32),
                pltpu.VMEM((cells, 2 * LANES), F32),
                pltpu.VMEM((GROUP, LANES), F32),
                pltpu.VMEM((GROUP, LANES), F32),
            ],
        ),
        compiler_params=pltpu.CompilerParams(vmem_limit_bytes=LIMIT),
        cost_estimate=pl.CostEstimate(flops=20 * 10**9, bytes_accessed=50 * 10**6, transcendentals=0),
        name="to_target",
    )(me, source, multipoles, arrived, target_rows, weights, own, parents, parent_of.reshape(1, cells), octant.reshape(1, cells), l2l_ops)

    return pl.pallas_call(
        lambda me, *refs: back_kernel(devices, reach, me, *refs),
        out_shape=jax.ShapeDtypeStruct((coeffs, cells), F32),
        in_specs=[smem(), vmem(), vmem(), vmem()],
        out_specs=vmem(),
        compiler_params=pltpu.CompilerParams(vmem_limit_bytes=LIMIT // 4),
        cost_estimate=pl.CostEstimate(flops=10**9, bytes_accessed=2 * 10**6, transcendentals=0),
        name="returned",
    )(me, base, back, exported)


def solution(mesh):
    placed = (
        P(None, ("gx", "gy")),
        P(None, ("gx", "gy")),
        P(),
        P(),
        P(("gx", "gy"), None, None),
        P(("gx", "gy"), None, None),
        P(("gx", "gy"), None, None),
        P(("gx", "gy"), None),
        P(("gx", "gy")),
        P(("gx", "gy")),
    )
    return jax.shard_map(
        shards, mesh=mesh, in_specs=placed, out_specs=P(None, ("gx", "gy")), check_vma=False
    )
```
